32 devices in a mesh: group: 2 (over y), ctx: 16 (over z, x, core).
Axes of the slice: x: 2, y: 2, z: 4, core: 2. Of those that a mesh axis runs over, the one named last changes fastest.
Arguments:
- queries: bfloat16 [4096, 8192], P(('group', 'ctx')), parts along dimension 0, may hold values from -5 to 5
- keys: bfloat16 [4096, 512], P(('group', 'ctx')), parts along dimension 0, may hold values from -5 to 5
- values: bfloat16 [4096, 512], P(('group', 'ctx')), parts along dimension 0, may hold values from -6 to 6
- outputs: bfloat16 [4096, 8192], P(('group', 'ctx')), parts along dimension 0, may hold values from -6 to 6
- d_out: bfloat16 [4096, 8192], P(('group', 'ctx')), parts along dimension 0, may hold values from -6 to 6
- lengths: int32 [16], P('group'), parts along dimension 0, may hold values from 1 to 512, 2048 in all
Outputs:
- d_queries: bfloat16 [4096, 8192], P(('group', 'ctx')), parts along dimension 0
- d_keys: bfloat16 [4096, 512], P(('group', 'ctx')), parts along dimension 0
- d_values: bfloat16 [4096, 512], P(('group', 'ctx')), parts along dimension 0
The draws below stay inside these ranges and needn't reach their ends.
There are 2 independent parts, one for each index of `group`. The reference program is written for one: setup_inputs(seed, part) draws one part's arguments, and reference() takes and returns one part's arrays. A program takes and returns all parts, laid end to end along the dimension named above; each array names one. Nothing has to cross between parts.
Inputs may be any that keep to these rules, and one draw needn't show every extreme that they name: Each document is at most 512 tokens long, and one document in every draw is exactly that long; the lengths sum to 2048.
All inputs are finite; a program needn't handle non-finite values.
Results may differ from the reference program's by a relative error of at most 0.0049.
Values may be sent and summed in bfloat16 or wider, within the bound.
No kernel may reach another device: no remote copies, remote signals or barrier semaphores. Data moves between devices by JAX's collectives and lax.ppermute only.
A program may use at most 128 MiB of HBM per device.

```python
import math
import jax
import jax.numpy as jnp
import numpy as np
from jax import lax

TOK_DEV = 128
HQ = 64
HK = 4
HD = 128
SPAN = 4
TOKENS = 2048
NDOC = 8


def draw_queries(key, part):
    key = jax.random.fold_in(key, 11)
    result = jnp.clip(jax.random.normal(key, (TOKENS, HQ * HD), jnp.float32), -4.5, 4.5)
    return result.astype(jnp.bfloat16)


def draw_keys(key, part):
    key = jax.random.fold_in(key, 23)
    result = jnp.clip(jax.random.normal(key, (TOKENS, HK * HD), jnp.float32), -4.5, 4.5)
    return result.astype(jnp.bfloat16)


def shard_levels(stream_key, dims, cuts, low, high):
    def one(axis_at, shards_of):
        draws = jax.random.uniform(jax.random.fold_in(jax.random.fold_in(stream_key, 6), axis_at), (shards_of,), jnp.float32, low / len(cuts), high / len(cuts))
        return jnp.repeat(jnp.exp(draws), dims[axis_at] // shards_of).reshape((-1,) + (1,) * (len(dims) - axis_at - 1))

    loudness = one(*cuts[0])
    for cut in cuts[1:]:
        loudness = loudness * one(*cut)
    return loudness


def length_profile(count, total, bound, slope):
    weights = [(1 << 20) // math.isqrt(standing ** slope) + 1 for standing in range(2, count + 1)]
    surplus, holding = total - bound - (count - 1), [1] * (count - 1)
    while surplus > 0:
        candidates = [i for i in range(count - 1) if holding[i] < bound]
        pool, budget = sum([weights[i] for i in candidates]), surplus
        for i in candidates:
            more = min(bound - holding[i], max(1, budget * weights[i] // pool), surplus)
            holding[i] = holding[i] + more
            surplus = surplus - more
    return np.array([bound] + holding)


def ragged(own_key, count, total, bound, skew):
    if count == 2:
        one = jax.random.randint(own_key, (), max(1, total - bound), min(bound, total - 1) + 1)
        return jnp.stack([one, total - one])
    sizes = jnp.asarray(length_profile(count, total, bound, skew), jnp.int32)
    pairs = (count - 1) // 2
    source_of, taker = sizes[1:1 + 2 * pairs:2], sizes[2:2 + 2 * pairs:2]
    room = jnp.minimum(source_of - 1, bound - taker)
    passed = jax.random.randint(jax.random.fold_in(own_key, 1), (pairs,), 0, 1 << 20) % (room + 1)
    sizes = sizes.at[1:1 + 2 * pairs:2].set(source_of - passed).at[2:2 + 2 * pairs:2].set(taker + passed)
    return sizes[jax.random.permutation(jax.random.fold_in(own_key, 2), count)]


def centred(key, shape, width, limit, cuts=(), held_as=jnp.bfloat16):
    values = width * jax.random.normal(key, shape, jnp.float32)
    if cuts:
        values = values * shard_levels(key, shape, cuts, -0.22, 0.18)
    return jnp.clip(values, -limit, limit).astype(held_as)


def setup_inputs(seed: int = 0, part: int = 0) -> dict:
    streams_of = jax.random.split(jax.random.key(seed), 7)
    part_keys = jax.random.split(jax.random.fold_in(streams_of[6], part), 7)
    queries = draw_queries(jax.random.fold_in(jax.random.fold_in(streams_of[6], part), 71), part)
    keys = draw_keys(jax.random.fold_in(jax.random.fold_in(streams_of[6], part), 71), part)
    values = centred(part_keys[2], (TOKENS, HK * HD), 1.0, 6.0, ((0, 16),))
    outputs = centred(part_keys[3], (TOKENS, HQ * HD), 1.0, 6.0, ((0, 16),))
    d_out = centred(part_keys[4], (TOKENS, HQ * HD), 1.0, 6.0, ((0, 16),))
    lengths = ragged(part_keys[5], NDOC, TOKENS, SPAN * TOK_DEV, 1).astype(jnp.int32)
    return {"queries": queries, "keys": keys, "values": values, "outputs": outputs, "d_out": d_out, "lengths": lengths}


def doc_index(ends, positions):
    return jnp.sum((ends[None, :] <= positions[:, None]).astype(jnp.int32), axis=1).astype(jnp.int32)


def reference(queries, keys, values, outputs, d_out, lengths):
    per_kv = HQ // HK
    factor = 1.0 / (HD ** 0.5)
    ends = jnp.cumsum(lengths).astype(jnp.int32)
    behind = SPAN * TOK_DEV
    window = behind + TOK_DEV
    key_pad = jnp.pad(keys.reshape(TOKENS, HK, HD), ((behind, 0), (0, 0), (0, 0)))
    value_pad = jnp.pad(values.reshape(TOKENS, HK, HD), ((behind, 0), (0, 0), (0, 0)))
    query_four = queries.reshape(TOKENS, HK, per_kv, HD)
    output_four = outputs.reshape(TOKENS, HK, per_kv, HD)
    grad_four = d_out.reshape(TOKENS, HK, per_kv, HD)

    def block(carry, block_index):
        key_grads, value_grads = carry
        start = (block_index * TOK_DEV).astype(jnp.int32)
        query_pos = start + jnp.arange(TOK_DEV, dtype=jnp.int32)
        key_pos = start - behind + jnp.arange(window, dtype=jnp.int32)
        visible = (key_pos[None, :] <= query_pos[:, None]) & (key_pos[None, :] >= 0)
        visible = visible & (doc_index(ends, query_pos)[:, None] == doc_index(ends, key_pos)[None, :])
        query_rows = lax.dynamic_slice_in_dim(query_four, start, TOK_DEV, 0).astype(jnp.float32)
        output_rows = lax.dynamic_slice_in_dim(output_four, start, TOK_DEV, 0).astype(jnp.float32)
        grad_rows = lax.dynamic_slice_in_dim(grad_four, start, TOK_DEV, 0).astype(jnp.float32)
        key_rows = lax.dynamic_slice_in_dim(key_pad, start, window, 0).astype(jnp.float32)
        value_rows = lax.dynamic_slice_in_dim(value_pad, start, window, 0).astype(jnp.float32)
        scores = jnp.einsum('tkgd,ukd->kgtu', query_rows, key_rows) * factor
        masked = jnp.where(visible, scores, -jnp.inf)
        row_top = jnp.max(masked, axis=-1, keepdims=True)
        log_total = row_top + jnp.log(jnp.sum(jnp.exp(masked - row_top), axis=-1, keepdims=True))
        probs = jnp.where(visible, jnp.exp(jnp.where(visible, scores - log_total, 0.0)), 0.0)
        probs_half = probs.astype(jnp.bfloat16)
        grad_probs = jnp.einsum('tkgd,ukd->kgtu', grad_rows, value_rows)
        delta = jnp.einsum('tkgd,tkgd->kgt', grad_rows, output_rows)[..., None]
        grad_scores = (factor * probs * (grad_probs - delta)).astype(jnp.bfloat16)
        grad_query = jnp.einsum('kgtu,ukd->tkgd', grad_scores.astype(jnp.float32), key_rows)
        grad_key = jnp.einsum('kgtu,tkgd->ukd', grad_scores.astype(jnp.float32), query_rows)
        grad_value = jnp.einsum('kgtu,tkgd->ukd', probs_half.astype(jnp.float32), grad_rows)
        old_keys = lax.dynamic_slice_in_dim(key_grads, start, window, 0)
        old_values = lax.dynamic_slice_in_dim(value_grads, start, window, 0)
        key_grads = lax.dynamic_update_slice_in_dim(key_grads, old_keys + grad_key, start, 0)
        value_grads = lax.dynamic_update_slice_in_dim(value_grads, old_values + grad_value, start, 0)
        return (key_grads, value_grads), grad_query.astype(jnp.bfloat16)

    empty = jnp.zeros((TOKENS + behind, HK, HD), jnp.float32)
    (key_grads, value_grads), grad_queries = lax.scan(block, (empty, empty), jnp.arange(TOKENS // TOK_DEV, dtype=jnp.int32))
    d_queries = grad_queries.reshape(TOKENS, HQ * HD)
    d_keys = key_grads[behind:].astype(jnp.bfloat16).reshape(TOKENS, HK * HD)
    d_values = value_grads[behind:].astype(jnp.bfloat16).reshape(TOKENS, HK * HD)
    return (d_queries, d_keys, d_values)
```

```python
import functools
import math

import jax
import jax.numpy as jnp
from jax import lax
from jax.experimental import pallas as pl
from jax.experimental.pallas import tpu as pltpu
from jax.sharding import PartitionSpec as P

HQ = 64
HK = 4
HD = 128
SPAN = 4
PER = HQ // HK
FACTOR = 1.0 / math.sqrt(HD)
LOG2E = math.log2(math.e)
F32 = jnp.float32
BF = jnp.bfloat16
NT = (((1,), (1,)), ((), ()))
NN = (((1,), (0,)), ((), ()))
MIB = 2**20


def dot(a, b, dims):
    return lax.dot_general(a, b, dims, preferred_element_type=F32)


def starts_row(len_ref, qpos):
    def step(j, c):
        end, start = c
        end = end + len_ref[j]
        return end, jnp.where(end <= qpos, end, start)

    return lax.fori_loop(0, len_ref.shape[0], step, (jnp.int32(0), jnp.zeros_like(qpos)))[1]


def main_kernel(len_ref, place_ref, q_ref, do_ref, delta_ref, *refs, heads):
    k_refs, v_refs = refs[0:5], refs[5:10]
    dq_ref, own_ref, far_ref, swap_ref = refs[10:14]
    kall, vall, kt, bias, acck, accv = refs[14:]
    rows = q_ref.shape[0]
    place = place_ref[0]
    core = place % 2
    dists = (0, SPAN, 2, 1 + 2 * core, 3 - 2 * core)
    for j in range(5):
        kall[j * rows : (j + 1) * rows, :] = k_refs[j][...]
        vall[j * rows : (j + 1) * rows, :] = v_refs[j][...]
    kt[...] = kall[...].astype(F32).T.astype(BF)
    u = lax.broadcasted_iota(jnp.int32, (rows, rows), 0)
    t = lax.broadcasted_iota(jnp.int32, (rows, rows), 1)
    tri = u <= t

    @pl.when(pl.program_id(0) == 0)
    def _():
        qpos = place * rows + lax.broadcasted_iota(jnp.int32, (1, rows), 1)
        start = starts_row(len_ref, qpos)
        for n in range(4):
            if n == 0:
                pos = jnp.where(tri, place * rows + u, (place - SPAN) * rows + u)
            else:
                pos = (place - dists[n + 1]) * rows + u
            bias[n * rows : (n + 1) * rows, :] = jnp.where(pos >= start, 0.0, -jnp.inf).astype(F32)

    def tile(x, n, c):
        if n == 0:
            return jnp.where(tri, x[0:rows, c], x[rows : 2 * rows, c])
        return x[(n + 1) * rows : (n + 2) * rows, c]

    for ch in range(PER // heads):
        hs = [ch * heads + i for i in range(heads)]
        q2 = jnp.concatenate([q_ref[:, h * HD : (h + 1) * HD] for h in hs], axis=0)
        do2 = jnp.concatenate([do_ref[:, h * HD : (h + 1) * HD] for h in hs], axis=0)
        s = dot(kall[...], q2, NT)
        dp = dot(vall[...], do2, NT)
        pb = [[None] * heads for _ in range(5)]
        db = [[None] * heads for _ in range(5)]
        for i, h in enumerate(hs):
            c = slice(i * rows, (i + 1) * rows)
            tiles = [tile(s, n, c) + bias[n * rows : (n + 1) * rows, :] for n in range(4)]
            top = jnp.max(functools.reduce(jnp.maximum, tiles), axis=0, keepdims=True)
            es = [jnp.exp2((x - top) * (FACTOR * LOG2E)) for x in tiles]
            rl = 1.0 / jnp.sum(functools.reduce(jnp.add, es), axis=0, keepdims=True)
            dl = delta_ref[h : h + 1, :]
            for n in range(4):
                p = es[n] * rl
                d = (FACTOR * p) * (tile(dp, n, c) - dl)
                if n == 0:
                    pb[0][i] = jnp.where(tri, p, 0.0).astype(BF)
                    pb[1][i] = jnp.where(tri, 0.0, p).astype(BF)
                    db[0][i] = jnp.where(tri, d, 0.0).astype(BF)
                    db[1][i] = jnp.where(tri, 0.0, d).astype(BF)
                else:
                    pb[n + 1][i] = p.astype(BF)
                    db[n + 1][i] = d.astype(BF)
        probs = jnp.concatenate([jnp.concatenate(r, axis=1) for r in pb], axis=0)
        grads = jnp.concatenate([jnp.concatenate(r, axis=1) for r in db], axis=0)
        dv = dot(probs, do2, NN)
        dk = dot(grads, q2, NN)
        if ch == 0:
            accv[...] = dv
            acck[...] = dk
        else:
            accv[...] += dv
            acck[...] += dk
        dqt = dot(kt[...], grads, NN)
        for i, h in enumerate(hs):
            dq_ref[:, h * HD : (h + 1) * HD] = dqt[:, i * rows : (i + 1) * rows].T.astype(BF)
    for w, acc in enumerate((acck, accv)):
        own_ref[w] = acc[0:rows, :]
        far_ref[w] = acc[rows : 2 * rows, :]
        far_ref[2 + w] = acc[2 * rows : 3 * rows, :]
        swap_ref[2 + w] = acc[3 * rows : 4 * rows, :].astype(BF)
        swap_ref[w] = acc[4 * rows : 5 * rows, :].astype(BF)


def main_call(lengths, place, q, do, delta, ks, vs, heads=4):
    rows = q.shape[0]
    big = pl.BlockSpec((rows, PER * HD), lambda g, *_: (0, g))
    small = pl.BlockSpec((rows, HD), lambda g, *_: (0, g))

    def part(n):
        return pl.BlockSpec((n, rows, HD), lambda g, *_: (0, 0, g))

    return pl.pallas_call(
        functools.partial(main_kernel, heads=heads),
        grid_spec=pltpu.PrefetchScalarGridSpec(
            num_scalar_prefetch=2,
            grid=(HK,),
            in_specs=[big, big, pl.BlockSpec((PER, rows), lambda g, *_: (g, 0))] + [small] * 10,
            out_specs=[big, part(2), part(4), part(4)],
            scratch_shapes=[
                pltpu.VMEM((5 * rows, HD), BF),
                pltpu.VMEM((5 * rows, HD), BF),
                pltpu.VMEM((HD, 5 * rows), BF),
                pltpu.VMEM((4 * rows, rows), F32),
                pltpu.VMEM((5 * rows, HD), F32),
                pltpu.VMEM((5 * rows, HD), F32),
            ],
        ),
        out_shape=[
            jax.ShapeDtypeStruct((rows, HQ * HD), BF),
            jax.ShapeDtypeStruct((2, rows, HK * HD), F32),
            jax.ShapeDtypeStruct((4, rows, HK * HD), F32),
            jax.ShapeDtypeStruct((4, rows, HK * HD), BF),
        ],
        compiler_params=pltpu.CompilerParams(vmem_limit_bytes=50 * MIB),
        name="main",
    )(lengths, place, q, do, delta, *ks, *vs)


def delta_kernel(o_ref, do_ref, out_ref):
    rows = o_ref.shape[0]
    lane = lax.broadcasted_iota(jnp.int32, (rows, HD), 1)
    acc = jnp.zeros((rows, HD), F32)
    for h in range(PER):
        c = slice(h * HD, (h + 1) * HD)
        col = jnp.sum(o_ref[:, c].astype(F32) * do_ref[:, c].astype(F32), axis=1, keepdims=True)
        acc = jnp.where(lane == h, col, acc)
    out_ref[...] = acc.T[0:PER, :]


def delta_call(o, do):
    rows = o.shape[0]
    big = pl.BlockSpec((rows, PER * HD), lambda g: (0, g))
    return pl.pallas_call(
        delta_kernel,
        grid=(HK,),
        in_specs=[big, big],
        out_specs=pl.BlockSpec((PER, rows), lambda g: (g, 0)),
        out_shape=jax.ShapeDtypeStruct((HQ, rows), F32),
        cost_estimate=pl.CostEstimate(flops=10**8, bytes_accessed=4 * MIB, transcendentals=0),
        name="delta",
    )(o, do)


def moved(x, by):
    size = lax.axis_size("ctx")
    return lax.ppermute(x, "ctx", [(i, i + by) for i in range(size) if 0 <= i + by < size])


def swapped(x):
    size = lax.axis_size("ctx")
    return lax.ppermute(x, "ctx", [(i, i ^ 1) for i in range(size)])


def on_device(queries, keys, values, outputs, d_out, lengths):
    rows = queries.shape[0]
    place = lax.axis_index("ctx").astype(jnp.int32)
    even = place % 2 == 0
    k4, k2 = moved(keys, 4), moved(keys, 2)
    v4, v2 = moved(values, 4), moved(values, 2)
    delta = delta_call(outputs, d_out)
    k2s, v2s = swapped(k2), swapped(v2)
    sel = swapped(jnp.where(even, jnp.stack([keys, values]), jnp.stack([k4, v4])))
    d_queries, own, far, swap = main_call(
        lengths,
        place.reshape(1),
        queries,
        d_out,
        delta,
        (keys, k4, k2, k2s, sel[0]),
        (values, v4, v2, v2s, sel[1]),
    )
    back = swapped(swap).astype(F32)
    near, mid = back[0:2], back[2:4]
    far4 = (far[0:2] + jnp.where(even, 0.0, near)).astype(BF)
    far2 = (far[2:4] + mid).astype(BF)
    got4, got2 = moved(far4, -4), moved(far2, -2)
    total = own + jnp.where(even, near, 0.0) + got4.astype(F32) + got2.astype(F32)
    total = total.astype(BF)
    return d_queries, total[0], total[1]


def solution(mesh):
    spec = P(("group", "ctx"), None)
    return jax.shard_map(
        on_device,
        mesh=mesh,
        in_specs=(spec,) * 5 + (P("group"),),
        out_specs=(spec,) * 3,
        check_vma=False,
    )
```

```python
import functools
import math

import jax
import jax.numpy as jnp
from jax import lax
from jax.experimental import pallas as pl
from jax.experimental.pallas import tpu as pltpu
from jax.sharding import PartitionSpec as P

HQ = 64
HK = 4
HD = 128
SPAN = 4
PER = HQ // HK
FACTOR = 1.0 / math.sqrt(HD)
LOG2E = math.log2(math.e)
F32 = jnp.float32
BF = jnp.bfloat16
NT = (((1,), (1,)), ((), ()))
NN = (((1,), (0,)), ((), ()))
MIB = 2**20


def dot(a, b, dims):
    return lax.dot_general(a, b, dims, preferred_element_type=F32)


def starts_row(len_ref, qpos):
    def step(j, c):
        end, start = c
        end = end + len_ref[j]
        return end, jnp.where(end <= qpos, end, start)

    return lax.fori_loop(0, len_ref.shape[0], step, (jnp.int32(0), jnp.zeros_like(qpos)))[1]


def main_kernel(len_ref, place_ref, q_ref, do_ref, delta_ref, *refs, heads, kept):
    kv_refs = refs[0:6]
    dq_ref, own_ref, far_ref, swap_ref = refs[6 + kept : 10 + kept]
    kall, vall, kt, bias, acck, accv = refs[10 + kept :]
    rows = q_ref.shape[0]
    place = place_ref[0]
    core = place % 2
    dists = (0, SPAN, 2, 1 + 2 * core, 3 - 2 * core)
    for j in range(5):
        pair = kv_refs[j][...]
        if j == 4:
            pair = jnp.where(core == 0, pair, kv_refs[5][...])
        kall[j * rows : (j + 1) * rows, :] = pair[:, :HD]
        vall[j * rows : (j + 1) * rows, :] = pair[:, HD:]
    kt[...] = kall[...].astype(F32).T.astype(BF)
    u = lax.broadcasted_iota(jnp.int32, (rows, rows), 0)
    t = lax.broadcasted_iota(jnp.int32, (rows, rows), 1)
    tri = u <= t

    @pl.when(pl.program_id(0) == 0)
    def _():
        qpos = place * rows + lax.broadcasted_iota(jnp.int32, (1, rows), 1)
        start = starts_row(len_ref, qpos)
        for n in range(4):
            if n == 0:
                pos = jnp.where(tri, place * rows + u, (place - SPAN) * rows + u)
            else:
                pos = (place - dists[n + 1]) * rows + u
            bias[n * rows : (n + 1) * rows, :] = jnp.where(pos >= start, 0.0, -jnp.inf).astype(F32)

    def tile(x, n, c):
        if n == 0:
            return jnp.where(tri, x[0:rows, c], x[rows : 2 * rows, c])
        return x[(n + 1) * rows : (n + 2) * rows, c]

    for ch in range(PER // heads):
        hs = [ch * heads + i for i in range(heads)]
        q2 = jnp.concatenate([q_ref[:, h * HD : (h + 1) * HD] for h in hs], axis=0)
        do2 = jnp.concatenate([do_ref[:, h * HD : (h + 1) * HD] for h in hs], axis=0)
        s = dot(kall[...], q2, NT)
        dp = dot(vall[...], do2, NT)
        pb = [[None] * heads for _ in range(5)]
        db = [[None] * heads for _ in range(5)]
        for i, h in enumerate(hs):
            c = slice(i * rows, (i + 1) * rows)
            tiles = [tile(s, n, c) + bias[n * rows : (n + 1) * rows, :] for n in range(4)]
            top = jnp.max(functools.reduce(jnp.maximum, tiles), axis=0, keepdims=True)
            es = [jnp.exp2((x - top) * (FACTOR * LOG2E)) for x in tiles]
            rl = 1.0 / jnp.sum(functools.reduce(jnp.add, es), axis=0, keepdims=True)
            dl = delta_ref[h : h + 1, :]
            for n in range(4):
                p = es[n] * rl
                d = (FACTOR * p) * (tile(dp, n, c) - dl)
                if n == 0:
                    pb[0][i] = jnp.where(tri, p, 0.0).astype(BF)
                    pb[1][i] = jnp.where(tri, 0.0, p).astype(BF)
                    db[0][i] = jnp.where(tri, d, 0.0).astype(BF)
                    db[1][i] = jnp.where(tri, 0.0, d).astype(BF)
                else:
                    pb[n + 1][i] = p.astype(BF)
                    db[n + 1][i] = d.astype(BF)
        probs = jnp.concatenate([jnp.concatenate(r, axis=1) for r in pb], axis=0)
        grads = jnp.concatenate([jnp.concatenate(r, axis=1) for r in db], axis=0)
        dv = dot(probs, do2, NN)
        dk = dot(grads, q2, NN)
        if ch == 0:
            accv[...] = dv
            acck[...] = dk
        else:
            accv[...] += dv
            acck[...] += dk
        dqt = dot(kt[...], grads, NN)
        for i, h in enumerate(hs):
            dq_ref[:, h * HD : (h + 1) * HD] = dqt[:, i * rows : (i + 1) * rows].T.astype(BF)
    for w, acc in enumerate((acck, accv)):
        c = slice(w * HD, (w + 1) * HD)
        own_ref[:, c] = acc[0:rows, :]
        far_ref[0, :, c] = acc[rows : 2 * rows, :]
        far_ref[1, :, c] = acc[2 * rows : 3 * rows, :]
        swap_ref[1, :, c] = acc[3 * rows : 4 * rows, :].astype(BF)
        swap_ref[0, :, c] = acc[4 * rows : 5 * rows, :].astype(BF)


def main_call(lengths, place, q, do, delta, kvs, dq, parts, first, last, local, base, width):
    rows = q.shape[0]
    big = pl.BlockSpec((rows, PER * HD), lambda g, *_: (0, first + g))
    pair = pl.BlockSpec((rows, 2 * HD), lambda g, *_: (0, local + g))
    own = pl.BlockSpec((rows, 2 * HD), lambda g, *_: (0, base + g))
    far = pl.BlockSpec((2, rows, 2 * HD), lambda g, *_: (0, 0, base + g))
    kept = [] if dq is None else [(0, dq)]
    kept += [] if parts is None else [(1 + i, x) for i, x in enumerate(parts)]
    return pl.pallas_call(
        functools.partial(main_kernel, heads=4, kept=len(kept)),
        grid_spec=pltpu.PrefetchScalarGridSpec(
            num_scalar_prefetch=2,
            grid=(last - first,),
            in_specs=[big, big, pl.BlockSpec((PER, rows), lambda g, *_: (first + g, 0))]
            + [pair] * 6
            + [pl.BlockSpec(memory_space=pl.ANY)] * len(kept),
            out_specs=[big, own, far, far],
            scratch_shapes=[
                pltpu.VMEM((5 * rows, HD), BF),
                pltpu.VMEM((5 * rows, HD), BF),
                pltpu.VMEM((HD, 5 * rows), BF),
                pltpu.VMEM((4 * rows, rows), F32),
                pltpu.VMEM((5 * rows, HD), F32),
                pltpu.VMEM((5 * rows, HD), F32),
            ],
        ),
        out_shape=[
            jax.ShapeDtypeStruct((rows, HQ * HD), BF),
            jax.ShapeDtypeStruct((rows, width * 2 * HD), F32),
            jax.ShapeDtypeStruct((2, rows, width * 2 * HD), F32),
            jax.ShapeDtypeStruct((2, rows, width * 2 * HD), BF),
        ],
        input_output_aliases={11 + i: o for i, (o, _) in enumerate(kept)},
        compiler_params=pltpu.CompilerParams(vmem_limit_bytes=58 * MIB),
        cost_estimate=pl.CostEstimate(
            flops=(last - first) * 5 * 10**9,
            bytes_accessed=(last - first) * 2 * MIB,
            transcendentals=(last - first) * 10**6,
        ),
        name="main",
    )(lengths, place, q, do, delta, *kvs, *[x for _, x in kept])


def delta_kernel(o_ref, do_ref, out_ref):
    rows = o_ref.shape[0]
    ones = jnp.ones((8, 2 * HD), BF)
    for h in range(PER):
        c = slice(h * HD, (h + 1) * HD)
        x = o_ref[:, c].astype(F32) * do_ref[:, c].astype(F32)
        high = x.astype(BF)
        low = (x - high.astype(F32)).astype(BF)
        out_ref[h : h + 1, :] = dot(ones, jnp.concatenate([high, low], axis=1), NT)[0:1, :]


def delta_call(o, do):
    rows = o.shape[0]
    big = pl.BlockSpec((rows, PER * HD), lambda g: (0, g))
    return pl.pallas_call(
        delta_kernel,
        grid=(HK,),
        in_specs=[big, big],
        out_specs=pl.BlockSpec((PER, rows), lambda g: (g, 0)),
        out_shape=jax.ShapeDtypeStruct((HQ, rows), F32),
        cost_estimate=pl.CostEstimate(flops=10**8, bytes_accessed=4 * MIB, transcendentals=0),
        name="delta",
    )(o, do)


def moved(x, by):
    size = lax.axis_size("ctx")
    return lax.ppermute(x, "ctx", [(i, (i + by) % size) for i in range(size)])


def swapped(x):
    size = lax.axis_size("ctx")
    return lax.ppermute(x, "ctx", [(i, i ^ 1) for i in range(size)])


def pack_kernel(k_ref, v_ref, *out_refs):
    at = 0
    for out_ref in out_refs:
        for i in range(out_ref.shape[1] // (2 * HD)):
            c = slice(at * HD, (at + 1) * HD)
            out_ref[:, 2 * i * HD : (2 * i + 1) * HD] = k_ref[:, c]
            out_ref[:, (2 * i + 1) * HD : (2 * i + 2) * HD] = v_ref[:, c]
            at += 1


def pack_call(keys, values):
    rows = keys.shape[0]
    return pl.pallas_call(
        pack_kernel,
        out_shape=[jax.ShapeDtypeStruct((rows, (e - f) * 2 * HD), BF) for f, e in FORTH],
        name="pack",
    )(keys, values)


def sum_kernel(place_ref, *refs):
    even = place_ref[0] % 2 == 0
    dk_ref, dv_ref = refs[-2:]
    at = 0
    for n in range(len(refs) // 4):
        mine, near, got4, got2 = refs[4 * n : 4 * n + 4]
        for i in range(mine.shape[1] // (2 * HD)):
            for w, out_ref in enumerate((dk_ref, dv_ref)):
                c = slice((2 * i + w) * HD, (2 * i + w + 1) * HD)
                total = mine[:, c] + jnp.where(even, near[0, :, c].astype(F32), 0.0)
                total = total + got4[:, c].astype(F32) + got2[:, c].astype(F32)
                out_ref[:, at * HD : (at + 1) * HD] = total.astype(BF)
            at += 1


def sum_call(index, sums):
    rows = sums[0].shape[0]
    return pl.pallas_call(
        sum_kernel,
        in_specs=[pl.BlockSpec(memory_space=pltpu.SMEM)] + [pl.BlockSpec(memory_space=pltpu.VMEM)] * len(sums),
        out_shape=[jax.ShapeDtypeStruct((rows, HK * HD), BF)] * 2,
        name="sum",
    )(index, *sums)


FORTH = ((0, 1), (1, 4))
CALLS = ((0, 1), (1, 2), (2, 4))
BACK = ((0, 2), (2, 4))


def on_device(queries, keys, values, outputs, d_out, lengths):
    place = lax.axis_index("ctx").astype(jnp.int32)
    even = place % 2 == 0
    index = place.reshape(1)
    own = pack_call(keys, values)
    two = [moved(x, 2) for x in own]
    four = [moved(x, 4) for x in own]
    mates = [swapped(x) for x in own]
    delta = delta_call(outputs, d_out)
    d_queries, sums, kvs, pending = None, [], None, None
    for first, end in BACK:
        parts = None
        for a, b in CALLS:
            if not first <= a < end:
                continue
            g = [f <= a < e for f, e in FORTH].index(True)
            if a == FORTH[g][0]:
                far, mid = four[g], two[g]
                if d_queries is not None:
                    far, mid, d_queries = lax.optimization_barrier((far, mid, d_queries))
                kvs = (own[g], far, mid, swapped(mid), swapped(far), mates[g])
            d_queries, *parts = main_call(
                lengths, index, queries, d_out, delta, kvs, d_queries, parts, a, b, a - FORTH[g][0], a - first, end - first
            )
        mine, far, swap = parts
        if pending is not None:
            swap, *pending = lax.optimization_barrier((swap, *pending))
            sums += pending
        back = swapped(swap)
        far4 = (far[0] + jnp.where(even, 0.0, back[0].astype(F32))).astype(BF)
        far2 = (far[1] + back[1].astype(F32)).astype(BF)
        if end < HK:
            far4, far2, d_queries = lax.optimization_barrier((far4, far2, d_queries))
        pending = (mine, back, moved(far4, -4), moved(far2, -2))
    d_keys, d_values = sum_call(index, (*sums, *pending))
    return d_queries, d_keys, d_values


def solution(mesh):
    spec = P(("group", "ctx"), None)
    return jax.shard_map(
        on_device,
        mesh=mesh,
        in_specs=(spec,) * 5 + (P("group"),),
        out_specs=(spec,) * 3,
        check_vma=False,
    )
```

```python
import functools
import math

import jax
import jax.numpy as jnp
from jax import lax
from jax.experimental import pallas as pl
from jax.experimental.pallas import tpu as pltpu
from jax.sharding import PartitionSpec as P

HQ = 64
HK = 4
HD = 128
SPAN = 4
PER = HQ // HK
FACTOR = 1.0 / math.sqrt(HD)
LOG2E = math.log2(math.e)
F32 = jnp.float32
BF = jnp.bfloat16
NT = (((1,), (1,)), ((), ()))
NN = (((1,), (0,)), ((), ()))
MIB = 2**20
CHUNK = 4
STEPS = 1
LATE_STEPS = 1


def dot(a, b, dims):
    return lax.dot_general(a, b, dims, preferred_element_type=F32)


def starts_row(len_ref, qpos):
    def step(j, c):
        end, start = c
        end = end + len_ref[j]
        return end, jnp.where(end <= qpos, end, start)

    return lax.fori_loop(0, len_ref.shape[0], step, (jnp.int32(0), jnp.zeros_like(qpos)))[1]


def stacked(ref, hs):
    return jnp.concatenate([ref[:, h * HD : (h + 1) * HD] for h in hs], axis=0)


def chunks(steps):
    return [list(range(i, i + CHUNK)) for i in range(0, PER // steps, CHUNK)]


def main_kernel(len_ref, place_ref, q_ref, do_ref, delta_ref, *refs):
    k_refs, v_refs = refs[0:6], refs[6:12]
    d_ref, p_ref, far_ref, swap_ref = refs[12:16]
    kall, vall, bias, acck, accv = refs[16:]
    rows = q_ref.shape[0]
    place = place_ref[0]
    core = place % 2
    dists = (SPAN, 2, 1 + 2 * core, 3 - 2 * core)
    u = lax.broadcasted_iota(jnp.int32, (rows, rows), 0)
    t = lax.broadcasted_iota(jnp.int32, (rows, rows), 1)
    tri = u <= t

    @pl.when((pl.program_id(0) == 0) & (pl.program_id(1) == 0))
    def _():
        start = starts_row(len_ref, place * rows + lax.broadcasted_iota(jnp.int32, (1, rows), 1))
        for n in range(4):
            pos = (place - dists[n]) * rows + u
            if n == 0:
                pos = jnp.where(tri, place * rows + u, pos)
            bias[n * rows : (n + 1) * rows, :] = jnp.where(pos >= start, 0.0, -jnp.inf).astype(F32)

    @pl.when(pl.program_id(1) == 0)
    def _():
        for all_ref, block_refs in ((kall, k_refs), (vall, v_refs)):
            for j in range(5):
                block = block_refs[j][...]
                if j == 4:
                    block = jnp.where(core == 0, block, block_refs[5][...])
                all_ref[j * rows : (j + 1) * rows, :] = block
        acck[...] = jnp.zeros_like(acck)
        accv[...] = jnp.zeros_like(accv)

    def tile(x, n, c):
        if n == 0:
            return jnp.where(tri, x[0:rows, c], x[rows : 2 * rows, c])
        return x[(n + 1) * rows : (n + 2) * rows, c]

    for hs in chunks(STEPS):
        q2 = stacked(q_ref, hs)
        do2 = stacked(do_ref, hs)
        s = dot(kall[...], q2, NT)
        dp = dot(vall[...], do2, NT)
        pb = [[None] * CHUNK for _ in range(4)]
        db = [[None] * CHUNK for _ in range(4)]
        for i, h in enumerate(hs):
            c = slice(i * rows, (i + 1) * rows)
            at = slice(h * rows, (h + 1) * rows)
            tiles = [tile(s, n, c) + bias[n * rows : (n + 1) * rows, :] for n in range(4)]
            top = jnp.max(functools.reduce(jnp.maximum, tiles), axis=0, keepdims=True)
            es = [jnp.exp2((x - top) * (FACTOR * LOG2E)) for x in tiles]
            rl = 1.0 / jnp.sum(functools.reduce(jnp.add, es), axis=0, keepdims=True)
            dl = delta_ref[pl.ds(pl.program_id(1) * (PER // STEPS) + h, 1), :]
            for n in range(4):
                p = es[n] * rl
                d = (FACTOR * p) * (tile(dp, n, c) - dl)
                if n == 0:
                    p_ref[:, at] = jnp.where(tri, p, 0.0).astype(BF)
                    d_ref[0:rows, at] = jnp.where(tri, d, 0.0).astype(BF)
                    p, d = jnp.where(tri, 0.0, p), jnp.where(tri, 0.0, d)
                pb[n][i] = p.astype(BF)
                db[n][i] = d.astype(BF)
        probs = jnp.concatenate([jnp.concatenate(r, axis=1) for r in pb], axis=0)
        grads = jnp.concatenate([jnp.concatenate(r, axis=1) for r in db], axis=0)
        d_ref[rows:, hs[0] * rows : (hs[-1] + 1) * rows] = grads
        accv[...] += dot(probs, do2, NN)
        acck[...] += dot(grads, q2, NN)

    @pl.when(pl.program_id(1) == STEPS - 1)
    def _():
        for w, acc in enumerate((acck, accv)):
            far_ref[w] = acc[0:rows, :]
            far_ref[2 + w] = acc[rows : 2 * rows, :]
            swap_ref[2 + w] = acc[2 * rows : 3 * rows, :].astype(BF)
            swap_ref[w] = acc[3 * rows : 4 * rows, :].astype(BF)


def specs(rows, steps):
    def wide(height):
        return pl.BlockSpec((height, PER // steps * HD), lambda g, i, *_: (0, g * steps + i))

    head = pl.BlockSpec((rows, HD), lambda g, i, *_: (0, g))

    def heads(n):
        return pl.BlockSpec((n, rows, HD), lambda g, i, *_: (0, 0, g))

    return wide, head, heads


def in_hbm(*xs):
    return [pltpu.with_memory_space_constraint(x, pltpu.HBM) for x in xs]


def main_call(lengths, index, q, do, delta, ks, vs):
    rows = q.shape[0]
    wide, head, heads = specs(rows, STEPS)
    return pl.pallas_call(
        main_kernel,
        grid_spec=pltpu.PrefetchScalarGridSpec(
            num_scalar_prefetch=2,
            grid=(HK, STEPS),
            in_specs=[wide(rows), wide(rows), pl.BlockSpec((PER, rows), lambda g, *_: (g, 0))] + [head] * 12,
            out_specs=[wide(5 * rows), wide(rows), heads(4), heads(4)],
            scratch_shapes=[
                pltpu.VMEM((5 * rows, HD), BF),
                pltpu.VMEM((5 * rows, HD), BF),
                pltpu.VMEM((4 * rows, rows), F32),
                pltpu.VMEM((4 * rows, HD), F32),
                pltpu.VMEM((4 * rows, HD), F32),
            ],
        ),
        out_shape=[
            pltpu.HBM((5 * rows, HQ * HD), BF),
            pltpu.HBM((rows, HQ * HD), BF),
            jax.ShapeDtypeStruct((4, rows, HK * HD), F32),
            jax.ShapeDtypeStruct((4, rows, HK * HD), BF),
        ],
        compiler_params=pltpu.CompilerParams(vmem_limit_bytes=40 * MIB),
        cost_estimate=pl.CostEstimate(flops=16 * 10**9, bytes_accessed=16 * MIB, transcendentals=4 * 10**6),
        name="main",
    )(lengths, index, *in_hbm(q, do, delta, *ks, *vs))


def late_kernel(place_ref, q_ref, do_ref, d_ref, p_ref, *refs):
    k_refs = refs[0:6]
    dq_ref, own_ref, kt = refs[6:]
    rows = q_ref.shape[0]
    core = place_ref[0] % 2

    @pl.when(pl.program_id(1) == 0)
    def _():
        for j in range(5):
            block = k_refs[j][...]
            if j == 4:
                block = jnp.where(core == 0, block, k_refs[5][...])
            kt[:, j * rows : (j + 1) * rows] = block.astype(F32).T.astype(BF)
        own_ref[...] = jnp.zeros_like(own_ref)

    for hs in chunks(LATE_STEPS):
        at = slice(hs[0] * rows, (hs[-1] + 1) * rows)
        dqt = dot(kt[...], d_ref[:, at], NN)
        for i, h in enumerate(hs):
            dq_ref[:, h * HD : (h + 1) * HD] = dqt[:, i * rows : (i + 1) * rows].T.astype(BF)
        own_ref[0] += dot(d_ref[0:rows, at], stacked(q_ref, hs), NN)
        own_ref[1] += dot(p_ref[:, at], stacked(do_ref, hs), NN)


def late_call(index, q, do, grads, probs, ks):
    rows = q.shape[0]
    wide, head, heads = specs(rows, LATE_STEPS)
    return pl.pallas_call(
        late_kernel,
        grid_spec=pltpu.PrefetchScalarGridSpec(
            num_scalar_prefetch=1,
            grid=(HK, LATE_STEPS),
            in_specs=[wide(rows), wide(rows), wide(5 * rows), wide(rows)] + [head] * 6,
            out_specs=[wide(rows), heads(2)],
            scratch_shapes=[pltpu.VMEM((HD, 5 * rows), BF)],
        ),
        out_shape=[jax.ShapeDtypeStruct((rows, HQ * HD), BF), jax.ShapeDtypeStruct((2, rows, HK * HD), F32)],
        compiler_params=pltpu.CompilerParams(vmem_limit_bytes=40 * MIB),
        cost_estimate=pl.CostEstimate(flops=8 * 10**9, bytes_accessed=20 * MIB, transcendentals=0),
        name="late",
    )(index, *in_hbm(q, do, grads, probs, *ks))


def delta_kernel(o_ref, do_ref, out_ref):
    rows = o_ref.shape[0]
    ones = jnp.ones((8, 2 * HD), BF)
    for h in range(PER):
        c = slice(h * HD, (h + 1) * HD)
        x = o_ref[:, c].astype(F32) * do_ref[:, c].astype(F32)
        high = x.astype(BF)
        low = (x - high.astype(F32)).astype(BF)
        out_ref[h : h + 1, :] = dot(ones, jnp.concatenate([high, low], axis=1), NT)[0:1, :]


def delta_call(o, do):
    rows = o.shape[0]
    big = pl.BlockSpec((rows, PER * HD), lambda g: (0, g))
    return pl.pallas_call(
        delta_kernel,
        grid=(HK,),
        in_specs=[big, big],
        out_specs=pl.BlockSpec((PER, rows), lambda g: (g, 0)),
        out_shape=jax.ShapeDtypeStruct((HQ, rows), F32),
        cost_estimate=pl.CostEstimate(flops=10**8, bytes_accessed=4 * MIB, transcendentals=0),
        name="delta",
    )(o, do)


def moved(x, by):
    size = lax.axis_size("ctx")
    return lax.ppermute(x, "ctx", [(i, (i + by) % size) for i in range(size)])


def swapped(x):
    size = lax.axis_size("ctx")
    return lax.ppermute(x, "ctx", [(i, i ^ 1) for i in range(size)])


def moved(x, by):
    size = lax.axis_size("ctx")
    return lax.ppermute(x, "ctx", [(i, (i + by) % size) for i in range(size)])


def swapped(x):
    size = lax.axis_size("ctx")
    return lax.ppermute(x, "ctx", [(i, i ^ 1) for i in range(size)])


def on_device(queries, keys, values, outputs, d_out, lengths):
    place = lax.axis_index("ctx").astype(jnp.int32)
    even = place % 2 == 0
    index = place.reshape(1)
    k2, k4 = moved(keys, 2), moved(keys, 4)
    v2, v4 = moved(values, 2), moved(values, 4)
    km, vm = swapped(keys), swapped(values)
    delta = delta_call(outputs, d_out)
    k2, k4, v2, v4, delta = lax.optimization_barrier((k2, k4, v2, v4, delta))
    ks = (keys, k4, k2, swapped(k2), swapped(k4), km)
    vs = (values, v4, v2, swapped(v2), swapped(v4), vm)
    grads, probs, far, swap = main_call(lengths, index, queries, d_out, delta, ks, vs)
    back = swapped(swap).astype(F32)
    near, mid = back[0:2], back[2:4]
    far4 = [(far[w] + jnp.where(even, 0.0, near[w])).astype(BF) for w in range(2)]
    far2 = [(far[2 + w] + mid[w]).astype(BF) for w in range(2)]
    index, *both = lax.optimization_barrier((index, *far4, *far2))
    got = [moved(x, -4 if i < 2 else -2).astype(F32) for i, x in enumerate(both)]
    d_queries, own = late_call(index, queries, d_out, grads, probs, ks)
    total = [(own[w] + jnp.where(even, near[w], 0.0) + got[w] + got[2 + w]).astype(BF) for w in range(2)]
    return d_queries, total[0], total[1]


def solution(mesh):
    spec = P(("group", "ctx"), None)
    return jax.shard_map(
        on_device,
        mesh=mesh,
        in_specs=(spec,) * 5 + (P("group"),),
        out_specs=(spec,) * 3,
        check_vma=False,
    )
```

```python
import functools
import math

import jax
import jax.numpy as jnp
from jax import lax
from jax.experimental import pallas as pl
from jax.experimental.pallas import tpu as pltpu
from jax.sharding import PartitionSpec as P

HQ = 64
HK = 4
HD = 128
SPAN = 4
PER = HQ // HK
FACTOR = 1.0 / math.sqrt(HD)
LOG2E = math.log2(math.e)
F32 = jnp.float32
BF = jnp.bfloat16
NT = (((1,), (1,)), ((), ()))
NN = (((1,), (0,)), ((), ()))
MIB = 2**20
CHUNK = 4
STEPS = 1
LATE_STEPS = 1


def dot(a, b, dims):
    return lax.dot_general(a, b, dims, preferred_element_type=F32)


def starts_row(len_ref, qpos):
    def step(j, c):
        end, start = c
        end = end + len_ref[j]
        return end, jnp.where(end <= qpos, end, start)

    return lax.fori_loop(0, len_ref.shape[0], step, (jnp.int32(0), jnp.zeros_like(qpos)))[1]


def stacked(ref, hs):
    return jnp.concatenate([ref[:, h * HD : (h + 1) * HD] for h in hs], axis=0)


def chunks(steps):
    return [list(range(i, i + CHUNK)) for i in range(0, PER // steps, CHUNK)]


def main_kernel(len_ref, place_ref, q_ref, do_ref, delta_ref, *refs):
    k_refs, v_refs = refs[0:6], refs[6:12]
    d_ref, p_ref, far_ref, swap_ref = refs[12:16]
    kall, vall, bias, acck, accv = refs[16:]
    rows = q_ref.shape[0]
    place = place_ref[0]
    core = place % 2
    dists = (SPAN, 2, 1 + 2 * core, 3 - 2 * core)
    u = lax.broadcasted_iota(jnp.int32, (rows, rows), 0)
    t = lax.broadcasted_iota(jnp.int32, (rows, rows), 1)
    tri = u <= t

    @pl.when((pl.program_id(0) == 0) & (pl.program_id(1) == 0))
    def _():
        start = starts_row(len_ref, place * rows + lax.broadcasted_iota(jnp.int32, (1, rows), 1))
        for n in range(4):
            pos = (place - dists[n]) * rows + u
            if n == 0:
                pos = jnp.where(tri, place * rows + u, pos)
            bias[n * rows : (n + 1) * rows, :] = jnp.where(pos >= start, 0.0, -jnp.inf).astype(F32)

    @pl.when(pl.program_id(1) == 0)
    def _():
        for all_ref, block_refs in ((kall, k_refs), (vall, v_refs)):
            for j in range(5):
                block = block_refs[j][...]
                if j == 4:
                    block = jnp.where(core == 0, block, block_refs[5][...])
                all_ref[j * rows : (j + 1) * rows, :] = block
        acck[...] = jnp.zeros_like(acck)
        accv[...] = jnp.zeros_like(accv)

    def tile(x, n, c):
        if n == 0:
            return jnp.where(tri, x[0:rows, c], x[rows : 2 * rows, c])
        return x[(n + 1) * rows : (n + 2) * rows, c]

    def products(hs):
        q2 = stacked(q_ref, hs)
        do2 = stacked(do_ref, hs)
        return q2, do2, dot(kall[...], q2, NT), dot(vall[...], do2, NT)

    def spread(ch, probs, grads, q2, do2):
        dv = dot(probs, do2, NN)
        dk = dot(grads, q2, NN)
        if ch == 0:
            accv[...] = dv
            acck[...] = dk
        else:
            accv[...] += dv
            acck[...] += dk

    todo = chunks(STEPS)
    ahead = products(todo[0])
    behind = None
    for ch, hs in enumerate(todo):
        q2, do2, s, dp = ahead
        if ch + 1 < len(todo):
            ahead = products(todo[ch + 1])
        pb = [[None] * CHUNK for _ in range(4)]
        db = [[None] * CHUNK for _ in range(4)]
        for i, h in enumerate(hs):
            c = slice(i * rows, (i + 1) * rows)
            at = slice(h * rows, (h + 1) * rows)
            tiles = [tile(s, n, c) + bias[n * rows : (n + 1) * rows, :] for n in range(4)]
            top = jnp.max(functools.reduce(jnp.maximum, tiles), axis=0, keepdims=True)
            es = [jnp.exp2((x - top) * (FACTOR * LOG2E)) for x in tiles]
            rl = 1.0 / jnp.sum(functools.reduce(jnp.add, es), axis=0, keepdims=True)
            dl = delta_ref[pl.ds(pl.program_id(1) * (PER // STEPS) + h, 1), :]
            for n in range(4):
                p = es[n] * rl
                d = (FACTOR * p) * (tile(dp, n, c) - dl)
                if n == 0:
                    p_ref[:, at] = jnp.where(tri, p, 0.0).astype(BF)
                    d_ref[0:rows, at] = jnp.where(tri, d, 0.0).astype(BF)
                    p, d = jnp.where(tri, 0.0, p), jnp.where(tri, 0.0, d)
                pb[n][i] = p.astype(BF)
                db[n][i] = d.astype(BF)
        probs = jnp.concatenate([jnp.concatenate(r, axis=1) for r in pb], axis=0)
        grads = jnp.concatenate([jnp.concatenate(r, axis=1) for r in db], axis=0)
        d_ref[rows:, hs[0] * rows : (hs[-1] + 1) * rows] = grads
        spread(ch, probs, grads, q2, do2)

    @pl.when(pl.program_id(1) == STEPS - 1)
    def _():
        for w, acc in enumerate((acck, accv)):
            far_ref[w] = acc[0:rows, :]
            far_ref[2 + w] = acc[rows : 2 * rows, :]
            swap_ref[2 + w] = acc[2 * rows : 3 * rows, :].astype(BF)
            swap_ref[w] = acc[3 * rows : 4 * rows, :].astype(BF)


def specs(rows, steps):
    def wide(height):
        return pl.BlockSpec((height, PER // steps * HD), lambda g, i, *_: (0, g * steps + i))

    head = pl.BlockSpec((rows, HD), lambda g, i, *_: (0, g))

    def heads(n):
        return pl.BlockSpec((n, rows, HD), lambda g, i, *_: (0, 0, g))

    return wide, head, heads


def in_hbm(*xs):
    return [pltpu.with_memory_space_constraint(x, pltpu.HBM) for x in xs]


def main_call(lengths, index, q, do, delta, ks, vs):
    rows = q.shape[0]
    wide, head, heads = specs(rows, STEPS)
    return pl.pallas_call(
        main_kernel,
        grid_spec=pltpu.PrefetchScalarGridSpec(
            num_scalar_prefetch=2,
            grid=(HK, STEPS),
            in_specs=[wide(rows), wide(rows), pl.BlockSpec((PER, rows), lambda g, *_: (g, 0))] + [head] * 12,
            out_specs=[wide(5 * rows), wide(rows), heads(4), heads(4)],
            scratch_shapes=[
                pltpu.VMEM((5 * rows, HD), BF),
                pltpu.VMEM((5 * rows, HD), BF),
                pltpu.VMEM((4 * rows, rows), F32),
                pltpu.VMEM((4 * rows, HD), F32),
                pltpu.VMEM((4 * rows, HD), F32),
            ],
        ),
        out_shape=[
            pltpu.HBM((5 * rows, HQ * HD), BF),
            pltpu.HBM((rows, HQ * HD), BF),
            jax.ShapeDtypeStruct((4, rows, HK * HD), F32),
            jax.ShapeDtypeStruct((4, rows, HK * HD), BF),
        ],
        compiler_params=pltpu.CompilerParams(vmem_limit_bytes=40 * MIB),
        cost_estimate=pl.CostEstimate(flops=16 * 10**9, bytes_accessed=16 * MIB, transcendentals=4 * 10**6),
        name="main",
    )(lengths, index, *in_hbm(q, do, delta, *ks, *vs))


def late_kernel(place_ref, q_ref, do_ref, d_ref, p_ref, *refs):
    k_refs = refs[0:6]
    dq_ref, own_ref, kt = refs[6:]
    rows = q_ref.shape[0]
    core = place_ref[0] % 2

    @pl.when(pl.program_id(1) == 0)
    def _():
        for j in range(5):
            block = k_refs[j][...]
            if j == 4:
                block = jnp.where(core == 0, block, k_refs[5][...])
            kt[:, j * rows : (j + 1) * rows] = block.astype(F32).T.astype(BF)
        own_ref[...] = jnp.zeros_like(own_ref)

    for hs in chunks(LATE_STEPS):
        at = slice(hs[0] * rows, (hs[-1] + 1) * rows)
        dqt = dot(kt[...], d_ref[:, at], NN)
        for i, h in enumerate(hs):
            dq_ref[:, h * HD : (h + 1) * HD] = dqt[:, i * rows : (i + 1) * rows].T.astype(BF)
        own_ref[0] += dot(d_ref[0:rows, at], stacked(q_ref, hs), NN)
        own_ref[1] += dot(p_ref[:, at], stacked(do_ref, hs), NN)


def late_call(index, q, do, grads, probs, ks):
    rows = q.shape[0]
    wide, head, heads = specs(rows, LATE_STEPS)
    return pl.pallas_call(
        late_kernel,
        grid_spec=pltpu.PrefetchScalarGridSpec(
            num_scalar_prefetch=1,
            grid=(HK, LATE_STEPS),
            in_specs=[wide(rows), wide(rows), wide(5 * rows), wide(rows)] + [head] * 6,
            out_specs=[wide(rows), heads(2)],
            scratch_shapes=[pltpu.VMEM((HD, 5 * rows), BF)],
        ),
        out_shape=[jax.ShapeDtypeStruct((rows, HQ * HD), BF), jax.ShapeDtypeStruct((2, rows, HK * HD), F32)],
        compiler_params=pltpu.CompilerParams(vmem_limit_bytes=40 * MIB),
        cost_estimate=pl.CostEstimate(flops=8 * 10**9, bytes_accessed=20 * MIB, transcendentals=0),
        name="late",
    )(index, *in_hbm(q, do, grads, probs, *ks))


def delta_kernel(o_ref, do_ref, out_ref):
    rows = o_ref.shape[0]
    ones = jnp.ones((8, 2 * HD), BF)
    for h in range(PER):
        c = slice(h * HD, (h + 1) * HD)
        x = o_ref[:, c].astype(F32) * do_ref[:, c].astype(F32)
        high = x.astype(BF)
        low = (x - high.astype(F32)).astype(BF)
        out_ref[h : h + 1, :] = dot(ones, jnp.concatenate([high, low], axis=1), NT)[0:1, :]


def delta_call(o, do):
    rows = o.shape[0]
    big = pl.BlockSpec((rows, PER * HD), lambda g: (0, g))
    return pl.pallas_call(
        delta_kernel,
        grid=(HK,),
        in_specs=[big, big],
        out_specs=pl.BlockSpec((PER, rows), lambda g: (g, 0)),
        out_shape=jax.ShapeDtypeStruct((HQ, rows), F32),
        cost_estimate=pl.CostEstimate(flops=10**8, bytes_accessed=4 * MIB, transcendentals=0),
        name="delta",
    )(o, do)


def moved(x, by):
    size = lax.axis_size("ctx")
    return lax.ppermute(x, "ctx", [(i, (i + by) % size) for i in range(size)])


def swapped(x):
    size = lax.axis_size("ctx")
    return lax.ppermute(x, "ctx", [(i, i ^ 1) for i in range(size)])


def moved(x, by):
    size = lax.axis_size("ctx")
    return lax.ppermute(x, "ctx", [(i, (i + by) % size) for i in range(size)])


def swapped(x):
    size = lax.axis_size("ctx")
    return lax.ppermute(x, "ctx", [(i, i ^ 1) for i in range(size)])


def on_device(queries, keys, values, outputs, d_out, lengths):
    place = lax.axis_index("ctx").astype(jnp.int32)
    even = place % 2 == 0
    index = place.reshape(1)
    k4 = moved(keys, 4)
    k2 = moved(keys, 2)
    v4 = moved(values, 4)
    v2 = moved(values, 2)
    km, vm = swapped(keys), swapped(values)
    delta = delta_call(outputs, d_out)
    k4, k2, delta = lax.optimization_barrier((k4, k2, delta))
    k2s, k4s = swapped(k2), swapped(k4)
    v4, v2, k2s, k4s = lax.optimization_barrier((v4, v2, k2s, k4s))
    ks = (keys, k4, k2, k2s, k4s, km)
    vs = (values, v4, v2, swapped(v2), swapped(v4), vm)
    grads, probs, far, swap = main_call(lengths, index, queries, d_out, delta, ks, vs)
    back = swapped(swap).astype(F32)
    near, mid = back[0:2], back[2:4]
    far4 = [(far[w] + jnp.where(even, 0.0, near[w])).astype(BF) for w in range(2)]
    far2 = [(far[2 + w] + mid[w]).astype(BF) for w in range(2)]
    index, *both = lax.optimization_barrier((index, *far4, *far2))
    got = [moved(x, -4 if i < 2 else -2).astype(F32) for i, x in enumerate(both)]
    d_queries, own = late_call(index, queries, d_out, grads, probs, ks)
    total = [(own[w] + jnp.where(even, near[w], 0.0) + got[w] + got[2 + w]).astype(BF) for w in range(2)]
    return d_queries, total[0], total[1]


def solution(mesh):
    spec = P(("group", "ctx"), None)
    return jax.shard_map(
        on_device,
        mesh=mesh,
        in_specs=(spec,) * 5 + (P("group"),),
        out_specs=(spec,) * 3,
        check_vma=False,
    )
```

```python
import functools
import math

import jax
import jax.numpy as jnp
from jax import lax
from jax.experimental import pallas as pl
from jax.experimental.pallas import tpu as pltpu
from jax.sharding import PartitionSpec as P

HQ = 64
HK = 4
HD = 128
SPAN = 4
PER = HQ // HK
FACTOR = 1.0 / math.sqrt(HD)
LOG2E = math.log2(math.e)
F32 = jnp.float32
BF = jnp.bfloat16
NT = (((1,), (1,)), ((), ()))
NN = (((1,), (0,)), ((), ()))
MIB = 2**20


def dot(a, b, dims):
    return lax.dot_general(a, b, dims, preferred_element_type=F32)


def starts_row(len_ref, qpos):
    def step(j, c):
        end, start = c
        end = end + len_ref[j]
        return end, jnp.where(end <= qpos, end, start)

    return lax.fori_loop(0, len_ref.shape[0], step, (jnp.int32(0), jnp.zeros_like(qpos)))[1]


GROUP = 8
CUTS = (0, 4, 8, 12, 15, 16)


def stacked(ref, half, hs):
    rows = ref.shape[0] // 2
    return jnp.concatenate([ref[half * rows : (half + 1) * rows, h * HD : (h + 1) * HD] for h in hs], axis=0)


def chunks():
    return [(half, list(range(i, i + GROUP))) for half in range(2) for i in range(0, PER, GROUP)]


def gathered(refs, core, half):
    blocks = [refs[j][...] for j in range(4)] + [jnp.where(core == 0, refs[4][...], refs[5][...])]
    rows = blocks[0].shape[0] // 2
    own, far = [(x[:rows], x[rows:]) for x in blocks[:2]]
    edge = [own[half], far[half], own[0] if half else far[1]]
    return jnp.concatenate(edge + blocks[2:], axis=0)


def main_kernel(len_ref, place_ref, q_ref, do_ref, delta_out_ref, *refs):
    k_refs, v_refs = refs[0:6], refs[6:12]
    d_out_ref, p_out_ref, far_ref, swap_ref = refs[12:16]
    kall, vall, bias, acck, accv, q_all, do_all, d_all, p_all, delta_ref, in_sems, out_sems, delta_sem = refs[16:]
    rows = q_ref.shape[0]
    part = rows // 2
    wide = GROUP * part

    def fetch(g):
        c = slice(g * PER * HD, PER * HD if g == 0 else HK * PER * HD)
        pairs = ((q_ref, q_all), (do_ref, do_all))
        return [pltpu.make_async_copy(x.at[:, c], y.at[:, c], in_sems.at[i, g]) for i, (x, y) in enumerate(pairs)]

    def store(n):
        c = slice(cuts[n] * wide, cuts[n + 1] * wide)
        pairs = ((d_all, d_out_ref), (p_all, p_out_ref))
        return [pltpu.make_async_copy(x.at[:, c], y.at[:, c], out_sems.at[i, n]) for i, (x, y) in enumerate(pairs)]

    cuts = CUTS

    rest = pltpu.make_async_copy(delta_out_ref, delta_ref, delta_sem)
    rest.start()
    for copy in fetch(0):
        copy.start()
    place = place_ref[0]
    core = place % 2
    dists = (2, 1 + 2 * core, 3 - 2 * core)
    tri = lax.broadcasted_iota(jnp.int32, (part, rows), 0) <= lax.broadcasted_iota(jnp.int32, (part, rows), 1) % part
    heights = [slice(0, part), slice(part, rows)] + [slice(n * rows, (n + 1) * rows) for n in (1, 2, 3)]

    u = lax.broadcasted_iota(jnp.int32, (part, rows), 0)
    whole = lax.broadcasted_iota(jnp.int32, (rows, rows), 0)
    lane = lax.broadcasted_iota(jnp.int32, (1, rows), 1) % part
    for half in range(2):
        start = starts_row(len_ref, place * rows + half * part + lane)
        at = half * part + u
        spots = [jnp.where(tri, place * rows + at, (place - SPAN) * rows + at)]
        spots += [place * rows + u if half else (place - SPAN) * rows + part + u]
        spots += [(place - n) * rows + whole for n in dists]
        for pos, c in zip(spots, heights):
            bias[half, c, :] = jnp.where(pos >= start, 0.0, -jnp.inf).astype(F32)
        kall[half] = gathered(k_refs, core, half)
        vall[half] = gathered(v_refs, core, half)

    def tiles_of(x, c):
        first = jnp.where(tri, x[0:part, c], x[part : 2 * part, c])
        cut = [slice(2 * part + x0, 2 * part + x1) for x0, x1 in ((0, part), (part, 3 * part), (3 * part, 5 * part), (5 * part, 7 * part))]
        return [first] + [x[y, c] for y in cut]

    def products(g, half, hs):
        c = slice(g * HD, (g + 1) * HD)
        hs = [g * PER + h for h in hs]
        q2 = stacked(q_all, half, hs)
        do2 = stacked(do_all, half, hs)
        return q2, do2, dot(kall[half, :, c], q2, NT), dot(vall[half, :, c], do2, NT)

    todo = [(g, *x) for g in range(HK) for x in chunks()]
    for copy in fetch(0):
        copy.wait()
    rest.wait()
    for copy in fetch(1):
        copy.start()
    ahead = products(*todo[0])
    for ch, (g, half, hs) in enumerate(todo):
        q2, do2, s, dp = ahead
        if g == 0 and todo[ch + 1][0] == 1:
            for copy in fetch(1):
                copy.wait()
        if ch + 1 < len(todo):
            ahead = products(*todo[ch + 1])
        pairs = len(hs) // 2
        pb = [[] for _ in range(6)]
        db = [[] for _ in range(6)]
        for i in range(pairs):
            c = slice(i * rows, (i + 1) * rows)
            tiles = [x + bias[half, y, :] for x, y in zip(tiles_of(s, c), heights)]
            top = functools.reduce(jnp.maximum, tiles[2:])
            edge = jnp.maximum(jnp.maximum(tiles[0], tiles[1]), jnp.maximum(top[:part], top[part:]))
            top = jnp.max(edge, axis=0, keepdims=True)
            es = [jnp.exp2((x - top) * (FACTOR * LOG2E)) for x in tiles]
            total = functools.reduce(jnp.add, es[2:])
            total = (es[0] + es[1]) + (total[:part] + total[part:])
            rl = 1.0 / jnp.sum(total, axis=0, keepdims=True)
            row = ch * pairs + i
            dl = delta_ref[row : row + 1, :]
            for n, (e, x) in enumerate(zip(es, tiles_of(dp, c))):
                p = e * rl
                d = (FACTOR * p) * (x - dl)
                if n == 0:
                    pb[0].append(jnp.where(tri, p, 0.0).astype(BF))
                    db[0].append(jnp.where(tri, d, 0.0).astype(BF))
                    p, d = jnp.where(tri, 0.0, p), jnp.where(tri, 0.0, d)
                pb[n + 1].append(p.astype(BF))
                db[n + 1].append(d.astype(BF))
        pb, db = [[jnp.concatenate(r, axis=1) for r in x] for x in (pb, db)]
        at = slice(ch * GROUP * part, (ch + 1) * GROUP * part)
        p_all[0:part, at] = pb[0]
        p_all[part:, at] = pb[2]
        d_all[:, at] = jnp.concatenate(db, axis=0)
        if ch + 1 in cuts:
            for copy in store(cuts.index(ch + 1) - 1):
                copy.start()
        send = [1, 3, 4, 5] if half else [1, 2, 3, 4, 5]
        to = slice(half * part, 4 * rows)
        c = slice(g * HD, (g + 1) * HD)
        dv = dot(jnp.concatenate([pb[n] for n in send], axis=0), do2, NN)
        dk = dot(jnp.concatenate([db[n] for n in send], axis=0), q2, NN)
        if todo[ch - 1][0] == g and ch > 0:
            accv[to, :] += dv
            acck[to, :] += dk
        else:
            accv[...] = dv
            acck[...] = dk
        if ch + 1 == len(todo) or todo[ch + 1][0] > g:
            for w, acc in enumerate((acck, accv)):
                far_ref[w, :, c] = acc[0:rows, :]
                far_ref[2 + w, :, c] = acc[rows : 2 * rows, :]
                swap_ref[2 + w, :, c] = acc[2 * rows : 3 * rows, :].astype(BF)
                swap_ref[w, :, c] = acc[3 * rows : 4 * rows, :].astype(BF)
    for n in range(len(cuts) - 1):
        for copy in store(n):
            copy.wait()


def specs(rows):
    def wide(height):
        return pl.BlockSpec((height, PER * HD), lambda g, *_: (0, g))

    def heads(n):
        return pl.BlockSpec((n, rows, HD), lambda g, *_: (0, 0, g))

    return wide, pl.BlockSpec((rows, HD), lambda g, *_: (0, g)), heads


def in_hbm(*xs):
    return [pltpu.with_memory_space_constraint(x, pltpu.HBM) for x in xs]


def main_call(lengths, index, q, do, delta, ks, vs):
    rows = q.shape[0]
    vmem, hbm = pl.BlockSpec(memory_space=pltpu.VMEM), pl.BlockSpec(memory_space=pltpu.HBM)
    smem = pl.BlockSpec(memory_space=pltpu.SMEM)
    tall = 9 * rows // 2
    return pl.pallas_call(
        main_kernel,
        in_specs=[smem, smem, hbm, hbm, hbm] + [vmem] * 12,
        out_specs=[hbm, hbm, vmem, vmem],
        scratch_shapes=[
            pltpu.VMEM((2, tall, HK * HD), BF),
            pltpu.VMEM((2, tall, HK * HD), BF),
            pltpu.VMEM((2, 4 * rows, rows), F32),
            pltpu.VMEM((4 * rows, HD), F32),
            pltpu.VMEM((4 * rows, HD), F32),
            pltpu.VMEM((rows, HQ * HD), BF),
            pltpu.VMEM((rows, HQ * HD), BF),
            pltpu.VMEM((tall, HQ * HD), BF),
            pltpu.VMEM((rows, HQ * HD), BF),
            pltpu.VMEM((HQ, rows), F32),
            pltpu.SemaphoreType.DMA((2, 2)),
            pltpu.SemaphoreType.DMA((2, len(CUTS) - 1)),
            pltpu.SemaphoreType.DMA,
        ],
        out_shape=[
            pltpu.HBM((tall, HQ * HD), BF),
            pltpu.HBM((rows, HQ * HD), BF),
            jax.ShapeDtypeStruct((4, rows, HK * HD), F32),
            jax.ShapeDtypeStruct((4, rows, HK * HD), BF),
        ],
        compiler_params=pltpu.CompilerParams(vmem_limit_bytes=40 * MIB),
        cost_estimate=pl.CostEstimate(flops=16 * 10**9, bytes_accessed=16 * MIB, transcendentals=4 * 10**6),
        name="main",
    )(lengths, index, *in_hbm(q, do, delta), *ks, *vs)


def late_kernel(place_ref, q_ref, do_ref, d_ref, p_ref, *refs):
    k_refs = refs[0:6]
    dq_ref, own_ref, kt = refs[6:]
    rows = q_ref.shape[0]
    part = rows // 2
    core = place_ref[0] % 2
    for half in range(2):
        kt[half] = gathered(k_refs, core, half).astype(F32).T.astype(BF)
    own_ref[...] = jnp.zeros_like(own_ref)
    for ch, (half, hs) in enumerate(chunks()):
        at = slice(ch * GROUP * part, (ch + 1) * GROUP * part)
        dqt = dot(kt[half], d_ref[:, at], NN)
        for i in range(GROUP // 2):
            pair = dqt[:, i * rows : (i + 1) * rows].T.astype(BF)
            for j in range(2):
                h = hs[2 * i + j]
                dq_ref[half * part : (half + 1) * part, h * HD : (h + 1) * HD] = pair[j * part : (j + 1) * part, :]
        grads, probs = d_ref[0:part, at], p_ref[0:part, at]
        if half:
            grads = jnp.concatenate([d_ref[rows : rows + part, at], grads], axis=0)
            probs = jnp.concatenate([p_ref[part:, at], probs], axis=0)
        to = slice(0, part + half * part)
        own_ref[0, to, :] += dot(grads, stacked(q_ref, half, hs), NN)
        own_ref[1, to, :] += dot(probs, stacked(do_ref, half, hs), NN)


def late_call(index, q, do, grads, probs, ks):
    rows = q.shape[0]
    wide, head, heads = specs(rows)
    return pl.pallas_call(
        late_kernel,
        grid_spec=pltpu.PrefetchScalarGridSpec(
            num_scalar_prefetch=1,
            grid=(HK,),
            in_specs=[wide(rows), wide(rows), wide(9 * rows // 2), wide(rows)] + [head] * 6,
            out_specs=[wide(rows), heads(2)],
            scratch_shapes=[pltpu.VMEM((2, HD, 9 * rows // 2), BF)],
        ),
        out_shape=[jax.ShapeDtypeStruct((rows, HQ * HD), BF), jax.ShapeDtypeStruct((2, rows, HK * HD), F32)],
        compiler_params=pltpu.CompilerParams(vmem_limit_bytes=40 * MIB),
        cost_estimate=pl.CostEstimate(flops=8 * 10**9, bytes_accessed=20 * MIB, transcendentals=0),
        name="late",
    )(index, *in_hbm(q, do, grads, probs), *ks)


def delta_kernel(o_ref, do_ref, out_ref):
    ones = jnp.ones((8, 2 * HD), BF)
    for ch, (half, hs) in enumerate(chunks()):
        for i in range(GROUP // 2):
            pair = hs[2 * i : 2 * i + 2]
            x = stacked(o_ref, half, pair).astype(F32) * stacked(do_ref, half, pair).astype(F32)
            high = x.astype(BF)
            low = (x - high.astype(F32)).astype(BF)
            row = ch * (GROUP // 2) + i
            out_ref[row : row + 1, :] = dot(ones, jnp.concatenate([high, low], axis=1), NT)[0:1, :]


def delta_call(o, do):
    rows = o.shape[0]
    big = pl.BlockSpec((rows, PER * HD), lambda g: (0, g))
    return pl.pallas_call(
        delta_kernel,
        grid=(HK,),
        in_specs=[big, big],
        out_specs=pl.BlockSpec((PER, rows), lambda g: (g, 0)),
        out_shape=jax.ShapeDtypeStruct((HQ, rows), F32),
        cost_estimate=pl.CostEstimate(flops=10**8, bytes_accessed=4 * MIB, transcendentals=0),
        name="delta",
    )(o, do)


def moved(x, by):
    size = lax.axis_size("ctx")
    return lax.ppermute(x, "ctx", [(i, (i + by) % size) for i in range(size)])


def swapped(x):
    size = lax.axis_size("ctx")
    return lax.ppermute(x, "ctx", [(i, i ^ 1) for i in range(size)])


def moved(x, by):
    size = lax.axis_size("ctx")
    return lax.ppermute(x, "ctx", [(i, (i + by) % size) for i in range(size)])


def swapped(x):
    size = lax.axis_size("ctx")
    return lax.ppermute(x, "ctx", [(i, i ^ 1) for i in range(size)])


def on_device(queries, keys, values, outputs, d_out, lengths):
    place = lax.axis_index("ctx").astype(jnp.int32)
    even = place % 2 == 0
    index = place.reshape(1)
    k4 = moved(keys, 4)
    k2 = moved(keys, 2)
    v4 = moved(values, 4)
    v2 = moved(values, 2)
    km, vm = swapped(keys), swapped(values)
    delta = delta_call(outputs, d_out)
    k4, k2, delta = lax.optimization_barrier((k4, k2, delta))
    k2s, k4s = swapped(k2), swapped(k4)
    v4, v2, k2s, k4s = lax.optimization_barrier((v4, v2, k2s, k4s))
    ks = (keys, k4, k2, k2s, k4s, km)
    vs = (values, v4, v2, swapped(v2), swapped(v4), vm)
    grads, probs, far, swap = main_call(lengths, index, queries, d_out, delta, ks, vs)
    back = swapped(swap).astype(F32)
    near, mid = back[0:2], back[2:4]
    far4 = [(far[w] + jnp.where(even, 0.0, near[w])).astype(BF) for w in range(2)]
    far2 = [(far[2 + w] + mid[w]).astype(BF) for w in range(2)]
    index, *both = lax.optimization_barrier((index, *far4, *far2))
    got = [moved(x, -4 if i < 2 else -2).astype(F32) for i, x in enumerate(both)]
    d_queries, own = late_call(index, queries, d_out, grads, probs, ks)
    total = [(own[w] + jnp.where(even, near[w], 0.0) + got[w] + got[2 + w]).astype(BF) for w in range(2)]
    return d_queries, total[0], total[1]


def solution(mesh):
    spec = P(("group", "ctx"), None)
    return jax.shard_map(
        on_device,
        mesh=mesh,
        in_specs=(spec,) * 5 + (P("group"),),
        out_specs=(spec,) * 3,
        check_vma=False,
    )
```

```python
import functools
import math

import jax
import jax.numpy as jnp
from jax import lax
from jax.experimental import pallas as pl
from jax.experimental.pallas import tpu as pltpu
from jax.sharding import PartitionSpec as P

HQ = 64
HK = 4
HD = 128
SPAN = 4
PER = HQ // HK
FACTOR = 1.0 / math.sqrt(HD)
LOG2E = math.log2(math.e)
F32 = jnp.float32
BF = jnp.bfloat16
NT = (((1,), (1,)), ((), ()))
NN = (((1,), (0,)), ((), ()))
MIB = 2**20


def dot(a, b, dims):
    return lax.dot_general(a, b, dims, preferred_element_type=F32)


def starts_row(len_ref, qpos):
    def step(j, c):
        end, start = c
        end = end + len_ref[j]
        return end, jnp.where(end <= qpos, end, start)

    return lax.fori_loop(0, len_ref.shape[0], step, (jnp.int32(0), jnp.zeros_like(qpos)))[1]


GROUP = 8
CUTS = (0, 4, 8, 12, 15, 16)


def stacked(ref, half, hs):
    rows = ref.shape[0] // 2
    return jnp.concatenate([ref[half * rows : (half + 1) * rows, h * HD : (h + 1) * HD] for h in hs], axis=0)


def chunks():
    return [(half, list(range(i, i + GROUP))) for half in range(2) for i in range(0, PER, GROUP)]


def gathered(refs, core, half):
    blocks = [refs[j][...] for j in range(4)] + [jnp.where(core == 0, refs[4][...], refs[5][...])]
    rows = blocks[0].shape[0] // 2
    own, far = [(x[:rows], x[rows:]) for x in blocks[:2]]
    edge = [own[half], far[half], own[0] if half else far[1]]
    return jnp.concatenate(edge + blocks[2:], axis=0)


def main_kernel(len_ref, place_ref, q_ref, do_ref, delta_out_ref, *refs):
    k_refs, v_refs = refs[0:6], refs[6:12]
    d_out_ref, p_out_ref, far_ref, swap_ref = refs[12:16]
    kall, vall, bias, acck, accv, q_all, do_all, d_all, p_all, delta_ref, in_sems, out_sems, delta_sem = refs[16:]
    rows = q_ref.shape[0]
    part = rows // 2
    wide = GROUP * part

    def fetch(g):
        c = slice(g * PER * HD, PER * HD if g == 0 else HK * PER * HD)
        pairs = ((q_ref, q_all), (do_ref, do_all))
        return [pltpu.make_async_copy(x.at[:, c], y.at[:, c], in_sems.at[i, g]) for i, (x, y) in enumerate(pairs)]

    def store(n):
        c = slice(cuts[n] * wide, cuts[n + 1] * wide)
        pairs = ((d_all, d_out_ref), (p_all, p_out_ref))
        return [pltpu.make_async_copy(x.at[:, c], y.at[:, c], out_sems.at[i, n]) for i, (x, y) in enumerate(pairs)]

    cuts = CUTS

    rest = pltpu.make_async_copy(delta_out_ref, delta_ref, delta_sem)
    rest.start()
    for copy in fetch(0):
        copy.start()
    place = place_ref[0]
    core = place % 2
    dists = (2, 1 + 2 * core, 3 - 2 * core)
    tri = lax.broadcasted_iota(jnp.int32, (part, rows), 0) <= lax.broadcasted_iota(jnp.int32, (part, rows), 1) % part
    heights = [slice(0, part), slice(part, rows)] + [slice(n * rows, (n + 1) * rows) for n in (1, 2, 3)]

    u = lax.broadcasted_iota(jnp.int32, (part, rows), 0)
    whole = lax.broadcasted_iota(jnp.int32, (rows, rows), 0)
    lane = lax.broadcasted_iota(jnp.int32, (1, rows), 1) % part
    for half in range(2):
        start = starts_row(len_ref, place * rows + half * part + lane)
        at = half * part + u
        spots = [jnp.where(tri, place * rows + at, (place - SPAN) * rows + at)]
        spots += [place * rows + u if half else (place - SPAN) * rows + part + u]
        spots += [(place - n) * rows + whole for n in dists]
        for pos, c in zip(spots, heights):
            bias[half, c, :] = jnp.where(pos >= start, 0.0, -jnp.inf).astype(F32)
        kall[half] = gathered(k_refs, core, half)
        vall[half] = gathered(v_refs, core, half)

    def tiles_of(x, c):
        first = jnp.where(tri, x[0:part, c], x[part : 2 * part, c])
        cut = [slice(2 * part + x0, 2 * part + x1) for x0, x1 in ((0, part), (part, 3 * part), (3 * part, 5 * part), (5 * part, 7 * part))]
        return [first] + [x[y, c] for y in cut]

    def products(g, half, hs):
        c = slice(g * HD, (g + 1) * HD)
        hs = [g * PER + h for h in hs]
        q2 = stacked(q_all, half, hs)
        do2 = stacked(do_all, half, hs)
        return q2, do2, dot(kall[half, :, c], q2, NT), dot(vall[half, :, c], do2, NT)

    behind = None

    def spread(ch, g, half, pb, db, q2, do2):
        send = [1, 3, 4, 5] if half else [1, 2, 3, 4, 5]
        to = slice(half * part, 4 * rows)
        c = slice(g * HD, (g + 1) * HD)
        dv = dot(jnp.concatenate([pb[n] for n in send], axis=0), do2, NN)
        dk = dot(jnp.concatenate([db[n] for n in send], axis=0), q2, NN)
        if todo[ch - 1][0] == g and ch > 0:
            accv[to, :] += dv
            acck[to, :] += dk
        else:
            accv[...] = dv
            acck[...] = dk
        if ch + 1 == len(todo) or todo[ch + 1][0] > g:
            for w, acc in enumerate((acck, accv)):
                far_ref[w, :, c] = acc[0:rows, :]
                far_ref[2 + w, :, c] = acc[rows : 2 * rows, :]
                swap_ref[2 + w, :, c] = acc[2 * rows : 3 * rows, :].astype(BF)
                swap_ref[w, :, c] = acc[3 * rows : 4 * rows, :].astype(BF)

    todo = [(g, *x) for g in range(HK) for x in chunks()]
    for copy in fetch(0):
        copy.wait()
    rest.wait()
    for copy in fetch(1):
        copy.start()
    ahead = products(*todo[0])
    for ch, (g, half, hs) in enumerate(todo):
        q2, do2, s, dp = ahead
        if g == 0 and todo[ch + 1][0] == 1:
            for copy in fetch(1):
                copy.wait()
        if ch + 1 < len(todo):
            ahead = products(*todo[ch + 1])
        pairs = len(hs) // 2
        pb = [[] for _ in range(6)]
        db = [[] for _ in range(6)]
        for i in range(pairs):
            c = slice(i * rows, (i + 1) * rows)
            tiles = [x + bias[half, y, :] for x, y in zip(tiles_of(s, c), heights)]
            top = functools.reduce(jnp.maximum, tiles[2:])
            edge = jnp.maximum(jnp.maximum(tiles[0], tiles[1]), jnp.maximum(top[:part], top[part:]))
            top = jnp.max(edge, axis=0, keepdims=True)
            es = [jnp.exp2((x - top) * (FACTOR * LOG2E)) for x in tiles]
            total = functools.reduce(jnp.add, es[2:])
            total = (es[0] + es[1]) + (total[:part] + total[part:])
            rl = 1.0 / jnp.sum(total, axis=0, keepdims=True)
            row = ch * pairs + i
            dl = delta_ref[row : row + 1, :]
            for n, (e, x) in enumerate(zip(es, tiles_of(dp, c))):
                p = e * rl
                d = (FACTOR * p) * (x - dl)
                if n == 0:
                    pb[0].append(jnp.where(tri, p, 0.0).astype(BF))
                    db[0].append(jnp.where(tri, d, 0.0).astype(BF))
                    p, d = jnp.where(tri, 0.0, p), jnp.where(tri, 0.0, d)
                pb[n + 1].append(p.astype(BF))
                db[n + 1].append(d.astype(BF))
        pb, db = [[jnp.concatenate(r, axis=1) for r in x] for x in (pb, db)]
        at = slice(ch * GROUP * part, (ch + 1) * GROUP * part)
        p_all[0:part, at] = pb[0]
        p_all[part:, at] = pb[2]
        d_all[:, at] = jnp.concatenate(db, axis=0)
        if ch + 1 in cuts:
            for copy in store(cuts.index(ch + 1) - 1):
                copy.start()
        if behind is not None:
            spread(*behind)
        behind = (ch, g, half, pb, db, q2, do2)
    spread(*behind)
    for n in range(len(cuts) - 1):
        for copy in store(n):
            copy.wait()


def specs(rows):
    def wide(height):
        return pl.BlockSpec((height, PER * HD), lambda g, *_: (0, g))

    def heads(n):
        return pl.BlockSpec((n, rows, HD), lambda g, *_: (0, 0, g))

    return wide, pl.BlockSpec((rows, HD), lambda g, *_: (0, g)), heads


def in_hbm(*xs):
    return [pltpu.with_memory_space_constraint(x, pltpu.HBM) for x in xs]


def main_call(lengths, index, q, do, delta, ks, vs):
    rows = q.shape[0]
    vmem, hbm = pl.BlockSpec(memory_space=pltpu.VMEM), pl.BlockSpec(memory_space=pltpu.HBM)
    smem = pl.BlockSpec(memory_space=pltpu.SMEM)
    tall = 9 * rows // 2
    return pl.pallas_call(
        main_kernel,
        in_specs=[smem, smem, hbm, hbm, hbm] + [vmem] * 12,
        out_specs=[hbm, hbm, vmem, vmem],
        scratch_shapes=[
            pltpu.VMEM((2, tall, HK * HD), BF),
            pltpu.VMEM((2, tall, HK * HD), BF),
            pltpu.VMEM((2, 4 * rows, rows), F32),
            pltpu.VMEM((4 * rows, HD), F32),
            pltpu.VMEM((4 * rows, HD), F32),
            pltpu.VMEM((rows, HQ * HD), BF),
            pltpu.VMEM((rows, HQ * HD), BF),
            pltpu.VMEM((tall, HQ * HD), BF),
            pltpu.VMEM((rows, HQ * HD), BF),
            pltpu.VMEM((HQ, rows), F32),
            pltpu.SemaphoreType.DMA((2, 2)),
            pltpu.SemaphoreType.DMA((2, len(CUTS) - 1)),
            pltpu.SemaphoreType.DMA,
        ],
        out_shape=[
            pltpu.HBM((tall, HQ * HD), BF),
            pltpu.HBM((rows, HQ * HD), BF),
            jax.ShapeDtypeStruct((4, rows, HK * HD), F32),
            jax.ShapeDtypeStruct((4, rows, HK * HD), BF),
        ],
        compiler_params=pltpu.CompilerParams(vmem_limit_bytes=40 * MIB),
        cost_estimate=pl.CostEstimate(flops=16 * 10**9, bytes_accessed=16 * MIB, transcendentals=4 * 10**6),
        name="main",
    )(lengths, index, *in_hbm(q, do, delta), *ks, *vs)


def late_kernel(place_ref, q_ref, do_ref, d_ref, p_ref, *refs):
    k_refs = refs[0:6]
    dq_ref, own_ref, kt = refs[6:]
    rows = q_ref.shape[0]
    part = rows // 2
    core = place_ref[0] % 2
    for half in range(2):
        kt[half] = gathered(k_refs, core, half).astype(F32).T.astype(BF)
    own_ref[...] = jnp.zeros_like(own_ref)
    for ch, (half, hs) in enumerate(chunks()):
        at = slice(ch * GROUP * part, (ch + 1) * GROUP * part)
        dqt = dot(kt[half], d_ref[:, at], NN)
        for i in range(GROUP // 2):
            pair = dqt[:, i * rows : (i + 1) * rows].T.astype(BF)
            for j in range(2):
                h = hs[2 * i + j]
                dq_ref[half * part : (half + 1) * part, h * HD : (h + 1) * HD] = pair[j * part : (j + 1) * part, :]
        grads, probs = d_ref[0:part, at], p_ref[0:part, at]
        if half:
            grads = jnp.concatenate([d_ref[rows : rows + part, at], grads], axis=0)
            probs = jnp.concatenate([p_ref[part:, at], probs], axis=0)
        to = slice(0, part + half * part)
        own_ref[0, to, :] += dot(grads, stacked(q_ref, half, hs), NN)
        own_ref[1, to, :] += dot(probs, stacked(do_ref, half, hs), NN)


def late_call(index, q, do, grads, probs, ks):
    rows = q.shape[0]
    wide, head, heads = specs(rows)
    return pl.pallas_call(
        late_kernel,
        grid_spec=pltpu.PrefetchScalarGridSpec(
            num_scalar_prefetch=1,
            grid=(HK,),
            in_specs=[wide(rows), wide(rows), wide(9 * rows // 2), wide(rows)] + [head] * 6,
            out_specs=[wide(rows), heads(2)],
            scratch_shapes=[pltpu.VMEM((2, HD, 9 * rows // 2), BF)],
        ),
        out_shape=[jax.ShapeDtypeStruct((rows, HQ * HD), BF), jax.ShapeDtypeStruct((2, rows, HK * HD), F32)],
        compiler_params=pltpu.CompilerParams(vmem_limit_bytes=40 * MIB),
        cost_estimate=pl.CostEstimate(flops=8 * 10**9, bytes_accessed=20 * MIB, transcendentals=0),
        name="late",
    )(index, *in_hbm(q, do, grads, probs), *ks)


def delta_kernel(o_ref, do_ref, out_ref):
    ones = jnp.ones((8, 2 * HD), BF)
    for ch, (half, hs) in enumerate(chunks()):
        for i in range(GROUP // 2):
            pair = hs[2 * i : 2 * i + 2]
            x = stacked(o_ref, half, pair).astype(F32) * stacked(do_ref, half, pair).astype(F32)
            high = x.astype(BF)
            low = (x - high.astype(F32)).astype(BF)
            row = ch * (GROUP // 2) + i
            out_ref[row : row + 1, :] = dot(ones, jnp.concatenate([high, low], axis=1), NT)[0:1, :]


def delta_call(o, do):
    rows = o.shape[0]
    big = pl.BlockSpec((rows, PER * HD), lambda g: (0, g))
    return pl.pallas_call(
        delta_kernel,
        grid=(HK,),
        in_specs=[big, big],
        out_specs=pl.BlockSpec((PER, rows), lambda g: (g, 0)),
        out_shape=jax.ShapeDtypeStruct((HQ, rows), F32),
        cost_estimate=pl.CostEstimate(flops=10**8, bytes_accessed=4 * MIB, transcendentals=0),
        name="delta",
    )(o, do)


def moved(x, by):
    size = lax.axis_size("ctx")
    return lax.ppermute(x, "ctx", [(i, (i + by) % size) for i in range(size)])


def swapped(x):
    size = lax.axis_size("ctx")
    return lax.ppermute(x, "ctx", [(i, i ^ 1) for i in range(size)])


def moved(x, by):
    size = lax.axis_size("ctx")
    return lax.ppermute(x, "ctx", [(i, (i + by) % size) for i in range(size)])


def swapped(x):
    size = lax.axis_size("ctx")
    return lax.ppermute(x, "ctx", [(i, i ^ 1) for i in range(size)])


def on_device(queries, keys, values, outputs, d_out, lengths):
    place = lax.axis_index("ctx").astype(jnp.int32)
    even = place % 2 == 0
    index = place.reshape(1)
    k4 = moved(keys, 4)
    k2 = moved(keys, 2)
    v4 = moved(values, 4)
    v2 = moved(values, 2)
    km, vm = swapped(keys), swapped(values)
    delta = delta_call(outputs, d_out)
    k4, k2, delta = lax.optimization_barrier((k4, k2, delta))
    k2s, k4s = swapped(k2), swapped(k4)
    v4, v2, k2s, k4s = lax.optimization_barrier((v4, v2, k2s, k4s))
    ks = (keys, k4, k2, k2s, k4s, km)
    vs = (values, v4, v2, swapped(v2), swapped(v4), vm)
    grads, probs, far, swap = main_call(lengths, index, queries, d_out, delta, ks, vs)
    back = swapped(swap).astype(F32)
    near, mid = back[0:2], back[2:4]
    far4 = [(far[w] + jnp.where(even, 0.0, near[w])).astype(BF) for w in range(2)]
    far2 = [(far[2 + w] + mid[w]).astype(BF) for w in range(2)]
    index, *both = lax.optimization_barrier((index, *far4, *far2))
    got = [moved(x, -4 if i < 2 else -2).astype(F32) for i, x in enumerate(both)]
    d_queries, own = late_call(index, queries, d_out, grads, probs, ks)
    total = [(own[w] + jnp.where(even, near[w], 0.0) + got[w] + got[2 + w]).astype(BF) for w in range(2)]
    return d_queries, total[0], total[1]


def solution(mesh):
    spec = P(("group", "ctx"), None)
    return jax.shard_map(
        on_device,
        mesh=mesh,
        in_specs=(spec,) * 5 + (P("group"),),
        out_specs=(spec,) * 3,
        check_vma=False,
    )
```

```python
import functools
import math

import jax
import jax.numpy as jnp
from jax import lax
from jax.experimental import pallas as pl
from jax.experimental.pallas import tpu as pltpu
from jax.sharding import PartitionSpec as P

HQ = 64
HK = 4
HD = 128
SPAN = 4
PER = HQ // HK
FACTOR = 1.0 / math.sqrt(HD)
LOG2E = math.log2(math.e)
F32 = jnp.float32
BF = jnp.bfloat16
NT = (((1,), (1,)), ((), ()))
NN = (((1,), (0,)), ((), ()))
MIB = 2**20


def dot(a, b, dims):
    return lax.dot_general(a, b, dims, preferred_element_type=F32)


def starts_row(len_ref, qpos):
    def step(j, c):
        end, start = c
        end = end + len_ref[j]
        return end, jnp.where(end <= qpos, end, start)

    return lax.fori_loop(0, len_ref.shape[0], step, (jnp.int32(0), jnp.zeros_like(qpos)))[1]


GROUP = 8
CUTS = (0, 4, 8, 12, 15, 16)


def stacked(ref, half, hs):
    rows = ref.shape[0] // 2
    return jnp.concatenate([ref[half * rows : (half + 1) * rows, h * HD : (h + 1) * HD] for h in hs], axis=0)


def chunks():
    return [(half, list(range(i, i + GROUP))) for half in range(2) for i in range(0, PER, GROUP)]


def gathered(refs, core, half):
    blocks = [refs[j][...] for j in range(4)] + [jnp.where(core == 0, refs[4][...], refs[5][...])]
    rows = blocks[0].shape[0] // 2
    own, far = [(x[:rows], x[rows:]) for x in blocks[:2]]
    edge = [own[half], far[half], own[0] if half else far[1]]
    return jnp.concatenate(edge + blocks[2:], axis=0)


def main_kernel(len_ref, place_ref, q_ref, do_ref, delta_out_ref, *refs):
    k_refs, v_refs = refs[0:6], refs[6:12]
    d_out_ref, p_out_ref, far_ref, swap_ref = refs[12:16]
    kall, vall, bias, acck, accv, q_all, do_all, d_all, p_all, delta_ref, in_sems, out_sems, delta_sem = refs[16:]
    rows = q_ref.shape[0]
    part = rows // 2
    wide = GROUP * part

    def fetch(g):
        c = slice(g * PER * HD, PER * HD if g == 0 else HK * PER * HD)
        pairs = ((q_ref, q_all), (do_ref, do_all))
        return [pltpu.make_async_copy(x.at[:, c], y.at[:, c], in_sems.at[i, g]) for i, (x, y) in enumerate(pairs)]

    def store(n):
        c = slice(cuts[n] * wide, cuts[n + 1] * wide)
        pairs = ((d_all, d_out_ref), (p_all, p_out_ref))
        return [pltpu.make_async_copy(x.at[:, c], y.at[:, c], out_sems.at[i, n]) for i, (x, y) in enumerate(pairs)]

    cuts = CUTS

    rest = pltpu.make_async_copy(delta_out_ref, delta_ref, delta_sem)
    rest.start()
    for copy in fetch(0):
        copy.start()
    place = place_ref[0]
    core = place % 2
    dists = (2, 1 + 2 * core, 3 - 2 * core)
    tri = lax.broadcasted_iota(jnp.int32, (part, rows), 0) <= lax.broadcasted_iota(jnp.int32, (part, rows), 1) % part
    heights = [slice(0, part), slice(part, rows)] + [slice(n * rows, (n + 1) * rows) for n in (1, 2, 3)]

    u = lax.broadcasted_iota(jnp.int32, (part, rows), 0)
    whole = lax.broadcasted_iota(jnp.int32, (rows, rows), 0)
    lane = lax.broadcasted_iota(jnp.int32, (1, rows), 1) % part
    for half in range(2):
        start = starts_row(len_ref, place * rows + half * part + lane)
        at = half * part + u
        spots = [jnp.where(tri, place * rows + at, (place - SPAN) * rows + at)]
        spots += [place * rows + u if half else (place - SPAN) * rows + part + u]
        spots += [(place - n) * rows + whole for n in dists]
        for pos, c in zip(spots, heights):
            bias[half, c, :] = jnp.where(pos >= start, 0.0, -jnp.inf).astype(F32)
        kall[half] = gathered(k_refs, core, half)
        vall[half] = gathered(v_refs, core, half)

    def tiles_of(x, c):
        first = jnp.where(tri, x[0:part, c], x[part : 2 * part, c])
        cut = [slice(2 * part + x0, 2 * part + x1) for x0, x1 in ((0, part), (part, 3 * part), (3 * part, 5 * part), (5 * part, 7 * part))]
        return [first] + [x[y, c] for y in cut]

    def products(g, half, hs):
        c = slice(g * HD, (g + 1) * HD)
        hs = [g * PER + h for h in hs]
        q2 = stacked(q_all, half, hs)
        do2 = stacked(do_all, half, hs)
        return q2, do2, dot(kall[half, :, c], q2, NT), dot(vall[half, :, c], do2, NT)

    behind = None

    def spread(ch, g, half, pb, db, q2, do2):
        send = [1, 3, 4, 5] if half else [1, 2, 3, 4, 5]
        to = slice(half * part, 4 * rows)
        c = slice(g * HD, (g + 1) * HD)
        dv = dot(jnp.concatenate([pb[n] for n in send], axis=0), do2, NN)
        dk = dot(jnp.concatenate([db[n] for n in send], axis=0), q2, NN)
        if todo[ch - 1][0] == g and ch > 0:
            accv[to, :] += dv
            acck[to, :] += dk
        else:
            accv[...] = dv
            acck[...] = dk
        if ch + 1 == len(todo) or todo[ch + 1][0] > g:
            for w, acc in enumerate((acck, accv)):
                far_ref[w, :, c] = acc[0:rows, :]
                far_ref[2 + w, :, c] = acc[rows : 2 * rows, :]
                swap_ref[2 + w, :, c] = acc[2 * rows : 3 * rows, :].astype(BF)
                swap_ref[w, :, c] = acc[3 * rows : 4 * rows, :].astype(BF)

    todo = [(g, *x) for g in range(HK) for x in chunks()]
    for copy in fetch(0):
        copy.wait()
    rest.wait()
    for copy in fetch(1):
        copy.start()
    ahead = products(*todo[0])
    for ch, (g, half, hs) in enumerate(todo):
        q2, do2, s, dp = ahead
        if g == 0 and todo[ch + 1][0] == 1:
            for copy in fetch(1):
                copy.wait()
        if ch + 1 < len(todo):
            ahead = products(*todo[ch + 1])
        pairs = len(hs) // 2
        pb = [[] for _ in range(6)]
        db = [[] for _ in range(6)]
        for i in range(pairs):
            c = slice(i * rows, (i + 1) * rows)
            tiles = [x + bias[half, y, :] for x, y in zip(tiles_of(s, c), heights)]
            top = functools.reduce(jnp.maximum, tiles[2:])
            edge = jnp.maximum(jnp.maximum(tiles[0], tiles[1]), jnp.maximum(top[:part], top[part:]))
            top = jnp.max(edge, axis=0, keepdims=True)
            es = [jnp.exp2((x - top) * (FACTOR * LOG2E)) for x in tiles]
            total = functools.reduce(jnp.add, es[2:])
            total = (es[0] + es[1]) + (total[:part] + total[part:])
            rl = 1.0 / jnp.sum(total, axis=0, keepdims=True)
            row = ch * pairs + i
            dl = delta_ref[row : row + 1, :]
            for n, (e, x) in enumerate(zip(es, tiles_of(dp, c))):
                p = e * rl
                d = (FACTOR * p) * (x - dl)
                if n == 0:
                    pb[0].append(jnp.where(tri, p, 0.0).astype(BF))
                    db[0].append(jnp.where(tri, d, 0.0).astype(BF))
                    p, d = jnp.where(tri, 0.0, p), jnp.where(tri, 0.0, d)
                pb[n + 1].append(p.astype(BF))
                db[n + 1].append(d.astype(BF))
        pb, db = [[jnp.concatenate(r, axis=1) for r in x] for x in (pb, db)]
        at = slice(ch * GROUP * part, (ch + 1) * GROUP * part)
        p_all[0:part, at] = pb[0]
        p_all[part:, at] = pb[2]
        d_all[:, at] = jnp.concatenate(db, axis=0)
        if ch + 1 in cuts:
            for copy in store(cuts.index(ch + 1) - 1):
                copy.start()
        if behind is not None:
            spread(*behind)
        behind = (ch, g, half, pb, db, q2, do2)
    spread(*behind)
    for n in range(len(cuts) - 1):
        for copy in store(n):
            copy.wait()


def specs(rows):
    def wide(height):
        return pl.BlockSpec((height, PER * HD), lambda g, *_: (0, g))

    def heads(n):
        return pl.BlockSpec((n, rows, HD), lambda g, *_: (0, 0, g))

    return wide, pl.BlockSpec((rows, HD), lambda g, *_: (0, g)), heads


def in_hbm(*xs):
    return [pltpu.with_memory_space_constraint(x, pltpu.HBM) for x in xs]


def main_call(lengths, index, q, do, delta, ks, vs):
    rows = q.shape[0]
    vmem, hbm = pl.BlockSpec(memory_space=pltpu.VMEM), pl.BlockSpec(memory_space=pltpu.HBM)
    smem = pl.BlockSpec(memory_space=pltpu.SMEM)
    tall = 9 * rows // 2
    return pl.pallas_call(
        main_kernel,
        in_specs=[smem, smem, hbm, hbm, hbm] + [vmem] * 12,
        out_specs=[hbm, hbm, vmem, vmem],
        scratch_shapes=[
            pltpu.VMEM((2, tall, HK * HD), BF),
            pltpu.VMEM((2, tall, HK * HD), BF),
            pltpu.VMEM((2, 4 * rows, rows), F32),
            pltpu.VMEM((4 * rows, HD), F32),
            pltpu.VMEM((4 * rows, HD), F32),
            pltpu.VMEM((rows, HQ * HD), BF),
            pltpu.VMEM((rows, HQ * HD), BF),
            pltpu.VMEM((tall, HQ * HD), BF),
            pltpu.VMEM((rows, HQ * HD), BF),
            pltpu.VMEM((HQ, rows), F32),
            pltpu.SemaphoreType.DMA((2, 2)),
            pltpu.SemaphoreType.DMA((2, len(CUTS) - 1)),
            pltpu.SemaphoreType.DMA,
        ],
        out_shape=[
            pltpu.HBM((tall, HQ * HD), BF),
            pltpu.HBM((rows, HQ * HD), BF),
            jax.ShapeDtypeStruct((4, rows, HK * HD), F32),
            jax.ShapeDtypeStruct((4, rows, HK * HD), BF),
        ],
        compiler_params=pltpu.CompilerParams(vmem_limit_bytes=40 * MIB),
        cost_estimate=pl.CostEstimate(flops=16 * 10**9, bytes_accessed=16 * MIB, transcendentals=4 * 10**6),
        name="main",
    )(lengths, index, *in_hbm(q, do, delta), *ks, *vs)


def late_kernel(place_ref, q_ref, do_ref, d_ref, p_ref, *refs):
    k_refs = refs[0:6]
    dq_ref, own_ref, kt = refs[6:]
    rows = q_ref.shape[0]
    part = rows // 2
    core = place_ref[0] % 2
    for half in range(2):
        kt[half] = gathered(k_refs, core, half).astype(F32).T.astype(BF)
    own_ref[...] = jnp.zeros_like(own_ref)
    for ch, (half, hs) in enumerate(chunks()):
        at = slice(ch * GROUP * part, (ch + 1) * GROUP * part)
        dqt = dot(kt[half], d_ref[:, at], NN)
        for i in range(GROUP // 2):
            pair = dqt[:, i * rows : (i + 1) * rows].T.astype(BF)
            for j in range(2):
                h = hs[2 * i + j]
                dq_ref[half * part : (half + 1) * part, h * HD : (h + 1) * HD] = pair[j * part : (j + 1) * part, :]
        grads, probs = d_ref[0:part, at], p_ref[0:part, at]
        if half:
            grads = jnp.concatenate([d_ref[rows : rows + part, at], grads], axis=0)
            probs = jnp.concatenate([p_ref[part:, at], probs], axis=0)
        to = slice(0, part + half * part)
        own_ref[0, to, :] += dot(grads, stacked(q_ref, half, hs), NN)
        own_ref[1, to, :] += dot(probs, stacked(do_ref, half, hs), NN)


def late_call(index, q, do, grads, probs, ks):
    rows = q.shape[0]
    wide, head, heads = specs(rows)
    return pl.pallas_call(
        late_kernel,
        grid_spec=pltpu.PrefetchScalarGridSpec(
            num_scalar_prefetch=1,
            grid=(HK,),
            in_specs=[wide(rows), wide(rows), wide(9 * rows // 2), wide(rows)] + [head] * 6,
            out_specs=[wide(rows), heads(2)],
            scratch_shapes=[pltpu.VMEM((2, HD, 9 * rows // 2), BF)],
        ),
        out_shape=[jax.ShapeDtypeStruct((rows, HQ * HD), BF), jax.ShapeDtypeStruct((2, rows, HK * HD), F32)],
        compiler_params=pltpu.CompilerParams(vmem_limit_bytes=40 * MIB),
        cost_estimate=pl.CostEstimate(flops=8 * 10**9, bytes_accessed=20 * MIB, transcendentals=0),
        name="late",
    )(index, *in_hbm(q, do, grads, probs), *ks)


def delta_kernel(o_ref, do_ref, out_ref):
    ones = jnp.ones((8, 2 * HD), BF)
    for ch, (half, hs) in enumerate(chunks()):
        for i in range(GROUP // 2):
            pair = hs[2 * i : 2 * i + 2]
            x = stacked(o_ref, half, pair).astype(F32) * stacked(do_ref, half, pair).astype(F32)
            high = x.astype(BF)
            low = (x - high.astype(F32)).astype(BF)
            row = ch * (GROUP // 2) + i
            out_ref[row : row + 1, :] = dot(ones, jnp.concatenate([high, low], axis=1), NT)[0:1, :]


def delta_call(o, do):
    rows = o.shape[0]
    big = pl.BlockSpec((rows, PER * HD), lambda g: (0, g))
    return pl.pallas_call(
        delta_kernel,
        grid=(HK,),
        in_specs=[big, big],
        out_specs=pl.BlockSpec((PER, rows), lambda g: (g, 0)),
        out_shape=jax.ShapeDtypeStruct((HQ, rows), F32),
        cost_estimate=pl.CostEstimate(flops=10**8, bytes_accessed=4 * MIB, transcendentals=0),
        name="delta",
    )(o, do)


def moved(x, by):
    size = lax.axis_size("ctx")
    return lax.ppermute(x, "ctx", [(i, (i + by) % size) for i in range(size)])


def swapped(x):
    size = lax.axis_size("ctx")
    return lax.ppermute(x, "ctx", [(i, i ^ 1) for i in range(size)])


def moved(x, by):
    size = lax.axis_size("ctx")
    return lax.ppermute(x, "ctx", [(i, (i + by) % size) for i in range(size)])


def swapped(x):
    size = lax.axis_size("ctx")
    return lax.ppermute(x, "ctx", [(i, i ^ 1) for i in range(size)])


def on_device(queries, keys, values, outputs, d_out, lengths):
    place = lax.axis_index("ctx").astype(jnp.int32)
    even = place % 2 == 0
    index = place.reshape(1)
    k4 = moved(keys, 4)
    k2 = moved(keys, 2)
    v4 = moved(values, 4)
    v2 = moved(values, 2)
    km, vm = swapped(keys), swapped(values)
    delta = delta_call(outputs, d_out)
    k4, k2, delta = lax.optimization_barrier((k4, k2, delta))
    k2s, k4s = swapped(k2), swapped(k4)
    v4, v2, k2s, k4s = lax.optimization_barrier((v4, v2, k2s, k4s))
    ks = (keys, k4, k2, k2s, k4s, km)
    vs = (values, v4, v2, swapped(v2), swapped(v4), vm)
    grads, probs, far, swap = main_call(lengths, index, queries, d_out, delta, ks, vs)
    back = swapped(swap)
    near, mid = back[0:2], back[2:4]
    far4 = [(far[w] + jnp.where(even, 0.0, near[w].astype(F32))).astype(BF) for w in range(2)]
    far2 = [(far[2 + w] + mid[w].astype(F32)).astype(BF) for w in range(2)]
    index, *both = lax.optimization_barrier((index, *far4, *far2))
    got = [moved(x, -4 if i < 2 else -2).astype(F32) for i, x in enumerate(both)]
    d_queries, own = late_call(index, queries, d_out, grads, probs, ks)
    total = [(own[w] + jnp.where(even, near[w].astype(F32), 0.0) + got[w] + got[2 + w]).astype(BF) for w in range(2)]
    return d_queries, total[0], total[1]


def solution(mesh):
    spec = P(("group", "ctx"), None)
    return jax.shard_map(
        on_device,
        mesh=mesh,
        in_specs=(spec,) * 5 + (P("group"),),
        out_specs=(spec,) * 3,
        check_vma=False,
    )
```
